512 devices in a mesh: dp: 8 (over x, z_hi), ctx: 64 (over y, z_lo, core).
Axes of the slice: x: 4, y: 4, z: 16 (z_hi: 2, z_lo: 8; z = z_hi * 8 + z_lo), core: 2. Of those that a mesh axis runs over, the one named last changes fastest.
Arguments:
- student_hidden: bfloat16 [131072, 1024], P(('dp', 'ctx'))
- w_query: bfloat16 [1024, 1024], P('dp'), may hold values from -0.5 to 0.5
- w_keyval: bfloat16 [1024, 512], P('dp'), may hold values from -0.1875 to 0.1875
- w_out: bfloat16 [1024, 1024], P('dp'), may hold values from -0.1875 to 0.1875
- norm_gain: float32 [1024], replicated, may hold values from 0.1 to 1.9
- student_head: float32 [1024], replicated, may hold values from -0.6 to 0.6
- teacher_query: bfloat16 [32, 2048], P('dp')
- teacher_keys: bfloat16 [131072, 2048], P(('dp', 'ctx')), may hold values from -6 to 6
- teacher_values: bfloat16 [131072, 2048], P(('dp', 'ctx')), may hold values from -6 to 6
- teacher_head: float32 [2048], replicated, may hold values from -0.125 to 0.125
- thread_lengths: int32 [32], replicated, may hold values from 1024 to 4096, as said below
- list_index: int32 [32], replicated, may hold values from 0 to 7, as said below
- relevance: int32 [32], replicated, may hold values from 0 to 3
Outputs:
- student_out: float32 [131072, 1024], P(('dp', 'ctx'))
- pooled: float32 [32, 1024], P('dp')
- teacher_score: float32 [32], P('dp')
- divergence: float32 [8], replicated
The draws below stay inside these ranges and needn't reach their ends.
Inputs may be any that keep to these rules, and one draw needn't show every extreme that they name: `thread_lengths`: each thread's valid tokens form its first rows; some thread is full and some has exactly 1024 valid tokens. `list_index`: each list holds exactly 4 threads.
All inputs are finite; a program needn't handle non-finite values.
Results may differ from the reference program's by a relative error of at most 0.007.
The reference program's roundings to bfloat16 on the way (of `query`, `keyval` and `attended`) count: a program that leaves them out, or rounds other values in their place, can miss the bound.
Values may be sent and summed in bfloat16 or wider, within the bound.
A program may use at most 128 MiB of HBM per device.

```python
import jax
import jax.numpy as jnp
from jax import lax

D_S = 1024
HEADS = 8
KV_HEADS = 2
HD = 128
T_HEADS = 16
TOK_DEV = 256
LENGTH = 4096
THREADS = 32
TOKENS = 131072
LISTS = 8


def draw_thread_lengths(key, part):
    key = jax.random.fold_in(key, 1)
    first, second = jax.random.split(key)
    base = jax.random.randint(first, (THREADS,), LENGTH // 4, LENGTH + 1)
    order = jax.random.permutation(second, THREADS)
    base = base.at[order[0]].set(LENGTH)
    base = base.at[order[1]].set(LENGTH // 4)
    return base.astype(jnp.int32)


def draw_list_index(key, part):
    key = jax.random.fold_in(key, 2)
    return (jax.random.permutation(key, THREADS) % LISTS).astype(jnp.int32)


def draw_student_hidden(key, part):
    key = jax.random.fold_in(key, 3)
    first, second = jax.random.split(key, 2)
    common = jax.random.normal(first, (THREADS, 1, D_S), jnp.float32)
    noise = jax.random.normal(second, (THREADS, LENGTH, D_S), jnp.float32)
    values = common * 0.3 + noise
    values = jnp.clip(values, -12.0, 12.0)
    return values.reshape(TOKENS, D_S).astype(jnp.bfloat16)


def draw_teacher_query(key, part):
    key = jax.random.fold_in(key, 4)
    first = jax.random.fold_in(key, 0)
    values = jax.random.normal(first, (THREADS, T_HEADS * HD), jnp.float32)
    rates = 2.0
    return jnp.clip(values * rates, -200.0, 200.0).astype(jnp.bfloat16)


def touch_ends(drawn, stream_key, smallest, top_value):
    longest = drawn.shape.index(max(drawn.shape))
    spots = []
    for shift in (0, 1):
        where = [jax.random.randint(jax.random.fold_in(stream_key, axis), (), 0, length) for axis, length in enumerate(drawn.shape)]
        where[longest] = (where[longest] + shift) % drawn.shape[longest]
        spots.append(tuple(where))
    return drawn.at[spots[0]].set(smallest).at[spots[1]].set(top_value)


def levels(rng, extent, cuts, low, high):
    def one(axis_at, shards_of):
        heights = jax.random.uniform(jax.random.fold_in(jax.random.fold_in(rng, 6), axis_at), (shards_of,), jnp.float32, low / len(cuts), high / len(cuts))
        return jnp.repeat(jnp.exp(heights), extent[axis_at] // shards_of).reshape((-1,) + (1,) * (len(extent) - axis_at - 1))

    factor_of = one(*cuts[0])
    for cut in cuts[1:]:
        factor_of = factor_of * one(*cut)
    return factor_of


def gaussian(stream_key, dims, spread, reach, shards=(), kind=jnp.bfloat16):
    values = jax.random.normal(stream_key, dims, jnp.float32) * spread
    if len(shards) > 0:
        values = levels(stream_key, dims, shards, -0.22, 0.18) * values
    return jnp.clip(values, min=-reach, max=reach).astype(kind)


def setup_inputs(seed: int = 0) -> dict:
    streams_of = jax.random.split(jax.random.key(seed), 14)
    student_hidden = draw_student_hidden(jax.random.fold_in(streams_of[13], 71), 0)
    w_query = gaussian(streams_of[1], (D_S, HEADS * HD), (D_S // 9) ** -0.5, 0.5, ((0, 8),))
    w_keyval = gaussian(streams_of[2], (D_S, 2 * KV_HEADS * HD), D_S ** -0.5, 0.1875, ((0, 8),))
    w_out = gaussian(streams_of[3], (HEADS * HD, D_S), (HEADS * HD) ** -0.5, 0.1875, ((0, 8),))
    norm_gain = jnp.clip(1.0 + 0.18 * jax.random.normal(streams_of[4], (D_S,), jnp.float32), 0.1, 1.9)
    student_head = gaussian(streams_of[5], (D_S,), 0.1, 0.6, (), jnp.float32)
    teacher_query = draw_teacher_query(jax.random.fold_in(streams_of[13], 71), 0)
    teacher_keys = gaussian(streams_of[7], (TOKENS, T_HEADS * HD), 1.0, 6.0, ((0, 512),))
    teacher_values = gaussian(streams_of[8], (TOKENS, T_HEADS * HD), 1.0, 6.0, ((0, 512),))
    teacher_head = gaussian(streams_of[9], (T_HEADS * HD,), (T_HEADS * HD) ** -0.5, 0.125, (), jnp.float32)
    thread_lengths = draw_thread_lengths(jax.random.fold_in(streams_of[13], 71), 0)
    list_index = draw_list_index(jax.random.fold_in(streams_of[13], 71), 0)
    relevance = touch_ends(jax.random.randint(streams_of[12], (THREADS,), 0, 4), jax.random.fold_in(streams_of[12], 1), 0, 3).astype(jnp.int32)
    return {"student_hidden": student_hidden, "w_query": w_query, "w_keyval": w_keyval, "w_out": w_out, "norm_gain": norm_gain, "student_head": student_head, "teacher_query": teacher_query, "teacher_keys": teacher_keys, "teacher_values": teacher_values, "teacher_head": teacher_head, "thread_lengths": thread_lengths, "list_index": list_index, "relevance": relevance}


def normalize(hidden, gain):
    return hidden * lax.rsqrt(lax.optimization_barrier(jnp.mean(hidden * hidden, axis=-1, keepdims=True)) + 1e-05) * gain

def list_divergence(teacher_score, student_score, list_index, relevance, lists):
    target = teacher_score + relevance.astype(jnp.float32)
    member = jnp.arange(lists)[:, None] == list_index[None, :]

    def log_soft(logits):
        masked = jnp.where(member, logits[None, :], -1e+30)
        top = lax.optimization_barrier(jnp.max(masked, axis=1, keepdims=True))
        shifted = jnp.where(member, jnp.exp(masked - top), 0.0)
        return masked - top - jnp.log(lax.optimization_barrier(jnp.sum(shifted, axis=1, keepdims=True)))
    target_log = log_soft(target)
    student_log = log_soft(student_score)
    target_prob = jnp.where(member, jnp.exp(target_log), 0.0)
    return lax.optimization_barrier(jnp.sum(jnp.where(member, target_prob * (target_log - student_log), 0.0), axis=1))

def reference(student_hidden, w_query, w_keyval, w_out, norm_gain, student_head, teacher_query, teacher_keys, teacher_values, teacher_head, thread_lengths, list_index, relevance):
    scale = HD ** (-0.5)
    groups = HEADS // KV_HEADS
    blocks = LENGTH // TOK_DEV
    positions = jnp.arange(LENGTH).astype(jnp.int32)

    def student_thread(args):
        hidden_in, length = args
        query = jnp.dot(hidden_in, w_query, preferred_element_type=jnp.float32).astype(jnp.bfloat16)
        keyval = jnp.dot(hidden_in, w_keyval, preferred_element_type=jnp.float32).astype(jnp.bfloat16)
        keys = keyval[:, :KV_HEADS * HD].reshape(LENGTH, KV_HEADS, HD).astype(jnp.float32)
        values = keyval[:, KV_HEADS * HD:].reshape(LENGTH, KV_HEADS, HD).astype(jnp.float32)
        query_blocks = query.reshape(blocks, TOK_DEV, KV_HEADS, groups, HD)

        def attend_block(args_block):
            block, start = args_block
            query_pos = start + jnp.arange(TOK_DEV).astype(jnp.int32)
            visible = (positions[None, :] <= query_pos[:, None])[:, None, None, :]
            scores = jnp.einsum('qkgd,tkd->qkgt', block.astype(jnp.float32), keys) * scale
            scores = jnp.where(visible, scores, -1e+30)
            best = lax.optimization_barrier(jnp.max(scores, axis=-1, keepdims=True))
            weights = jnp.where(visible, jnp.exp(scores - best), 0.0)
            total = lax.optimization_barrier(jnp.sum(weights, axis=-1))
            rounded = lax.optimization_barrier(weights.astype(jnp.bfloat16)).astype(jnp.float32)
            out = jnp.einsum('qkgt,tkd->qkgd', rounded, values) / total[..., None]
            return out.reshape(TOK_DEV, HEADS * HD).astype(jnp.bfloat16)
        starts = (jnp.arange(blocks) * TOK_DEV).astype(jnp.int32)
        attended = lax.map(attend_block, (query_blocks, starts)).reshape(LENGTH, HEADS * HD)
        hidden = hidden_in.astype(jnp.float32) + jnp.dot(attended, w_out, preferred_element_type=jnp.float32)
        valid = positions < length
        out = jnp.where(valid[:, None], hidden, 0.0)
        normed = normalize(hidden, norm_gain)
        pooled = lax.optimization_barrier(jnp.sum(jnp.where(valid[:, None], normed, 0.0), axis=0)) / length.astype(jnp.float32)
        return (out, pooled)
    hidden_threads = student_hidden.reshape(THREADS, LENGTH, D_S)
    outs, pooled = lax.map(student_thread, (hidden_threads, thread_lengths))
    student_out = outs.reshape(TOKENS, D_S)
    student_score = lax.optimization_barrier(jnp.sum(pooled * student_head[None, :], axis=1))

    def teacher_thread(args):
        tq, tk, tv, length = args
        q = tq.reshape(T_HEADS, HD).astype(jnp.float32)
        k = tk.reshape(LENGTH, T_HEADS, HD).astype(jnp.float32)
        v = tv.reshape(LENGTH, T_HEADS, HD).astype(jnp.float32)
        seen = (positions < length)[None, :]
        scores = jnp.einsum('hd,thd->ht', q, k) * scale
        scores = jnp.where(seen, scores, -1e+30)
        best = lax.optimization_barrier(jnp.max(scores, axis=-1, keepdims=True))
        weights = jnp.where(seen, jnp.exp(scores - best), 0.0)
        total = lax.optimization_barrier(jnp.sum(weights, axis=-1))
        rounded = lax.optimization_barrier(weights.astype(jnp.bfloat16)).astype(jnp.float32)
        out = jnp.einsum('ht,thd->hd', rounded, v) / total[:, None]
        return jnp.sum(out.reshape(-1) * teacher_head)
    teacher_score = lax.map(teacher_thread, (teacher_query, teacher_keys.reshape(THREADS, LENGTH, T_HEADS * HD), teacher_values.reshape(THREADS, LENGTH, T_HEADS * HD), thread_lengths))
    divergence = list_divergence(teacher_score, student_score, list_index, relevance, LISTS)
    return (student_out, pooled, teacher_score, divergence)
```

```python
import functools

import jax
import jax.numpy as jnp
from jax import lax
from jax.experimental import pallas as pl
from jax.experimental.pallas import tpu as pltpu
from jax.sharding import PartitionSpec as P

HEADS = 8
KV_HEADS = 2
GROUPS = 4
HD = 128
T_HEADS = 16
ROWS = 256
D = 1024
CHIPS = 8
BIG = -1e30
F32 = jnp.float32
BF16 = jnp.bfloat16
SCALE = HD ** (-0.5)
LOG2E = 1.4426950408889634
MESH = pl.DeviceIdType.MESH


def kernel(
    hid_in, wkv_in, wq_in, wo_in, gain_in, shead_in, tq_in, tk_in, tv_in, thead_in, len_in, list_in, rel_in,
    out_ref, pooled_ref, tscore_ref, div_ref,
    hid, wkv, wq, wo, tk, tv, kvb, relay, qt, att, m_ref, l_ref, acc_ref,
    tbuf, chain, cstage, pbuf, ybuf, dbuf,
    gain_ref, shead_ref, tq_ref, thead_ref, len_ref, list_ref, rel_ref,
    lsem, wsend, wrecv, kv_recv, kv_send, sib_send, rev_send, relay_recv, relay_send,
    t_send, t_recv, c_send, c_recv, p_send, p_recv, y_send, y_recv, d_send, d_recv,
):
    dp = lax.axis_index("dp")
    ctx = lax.axis_index("ctx")
    x, zh = dp // 2, dp % 2
    y, pos = ctx // 16, ctx % 16
    c, k = pos // 2, pos % 2
    oz = 1 - zh
    other_dp = 2 * x + oz
    sib_ctx = ctx + 1 - 2 * k
    line = y * 16

    def remote(src, dst, ssem, rsem, to_dp, to_ctx):
        return pltpu.make_async_remote_copy(
            src_ref=src, dst_ref=dst, send_sem=ssem, recv_sem=rsem, device_id=(to_dp, to_ctx), device_id_type=MESH
        )

    def x_peer(d):
        return 2 * ((x + d) % 4) + zh

    def y_peer(d):
        return ((y + d) % 4) * 16 + pos

    lane = 64 * k
    locals_ = [
        pltpu.make_async_copy(hid_in, hid, lsem.at[0]),
        pltpu.make_async_copy(tk_in, tk, lsem.at[1]),
        pltpu.make_async_copy(tv_in, tv, lsem.at[2]),
    ]
    weights = [(wkv_in, wkv), (wq_in, wq), (wo_in, wo)]
    for i, (w_in, w) in enumerate(weights):
        locals_.append(
            pltpu.make_async_copy(w_in.at[pl.ds(lane, 64)], w.at[x, zh, pl.ds(lane, 64)], lsem.at[3 + i])
        )
    small = [
        (gain_in, gain_ref), (shead_in, shead_ref), (tq_in, tq_ref), (thead_in, thead_ref), (len_in, len_ref),
        (list_in, list_ref), (rel_in, rel_ref),
    ]
    small = [pltpu.make_async_copy(src, dst, lsem.at[6 + i]) for i, (src, dst) in enumerate(small)]
    for copy in (locals_[0], locals_[3], locals_[1], locals_[2], locals_[4], locals_[5]):
        copy.start()
    for copy in small:
        copy.start()

    barrier = pltpu.get_barrier_semaphore()

    def greet(to_dp, to_ctx):
        pl.semaphore_signal(barrier, inc=1, device_id=(to_dp, to_ctx), device_id_type=MESH)

    for d in range(1, 16):
        greet(dp, line + (pos + d) % 16)
    for d in range(1, 4):
        greet(dp, y_peer(d))
    for d in range(1, 8):
        greet((dp + d) % 8, ctx)

    @pl.when(c == 0)
    def _():
        for j in range(4, 8):
            greet(other_dp, line + 2 * j + k)

    @pl.when(c == 7)
    def _():
        for j in range(4):
            greet(other_dp, line + 2 * j + k)

    @pl.when(jnp.logical_and(c >= 1, c <= 3))
    def _():
        greet(other_dp, line + 14 + k)

    @pl.when(jnp.logical_and(c >= 4, c <= 6))
    def _():
        greet(other_dp, line + k)

    pl.semaphore_wait(barrier, 26 + 3 * (c // 7 + 1 - (c + 6) // 7))

    class Gather:
        def __init__(self, i):
            self.i = i
            self.w_in, self.w = weights[i]
            self.piece = 64 * k + 16 * y

        def sem(self, table, n):
            return table.at[self.i, n]

        def z_copy(self, j):
            w = self.w.at[x, zh, pl.ds(self.piece, 16)]
            return remote(
                self.w_in.at[pl.ds(self.piece, 16)], w, self.sem(wsend, j % 4), self.sem(wrecv, 0),
                other_dp, line + 2 * j + k,
            )

        def z_start(self):
            @pl.when(c == 0)
            def _():
                for j in range(4, 8):
                    self.z_copy(j).start()

            @pl.when(c == 7)
            def _():
                for j in range(4):
                    self.z_copy(j).start()

        def z_recv(self):
            w = self.w.at[x, oz, pl.ds(self.piece, 16)]
            remote(w, w, self.sem(wsend, 0), self.sem(wrecv, 0), other_dp, ctx).wait_recv()

        def own_copy(self, d):
            return remote(
                self.w_in.at[pl.ds(lane, 64)], self.w.at[x, zh, pl.ds(lane, 64)],
                self.sem(wsend, 3 + d), self.sem(wrecv, d), x_peer(d), ctx,
            )

        def own_start(self):
            for d in range(1, 4):
                self.own_copy(d).start()

        def own_recv(self):
            for d in range(1, 4):
                w = self.w.at[(x + 4 - d) % 4, zh, pl.ds(lane, 64)]
                remote(w, w, self.sem(wsend, 0), self.sem(wrecv, d), dp, ctx).wait_recv()

        def other_copy(self, d):
            w = self.w.at[x, oz, pl.ds(self.piece, 16)]
            return remote(w, w, self.sem(wsend, 6 + d), self.sem(wrecv, 3 + d), x_peer(d), ctx)

        def other_start(self):
            for d in range(1, 4):
                self.other_copy(d).start()

        def other_recv(self):
            for d in range(1, 4):
                w = self.w.at[(x + 4 - d) % 4, oz, pl.ds(self.piece, 16)]
                remote(w, w, self.sem(wsend, 0), self.sem(wrecv, 3 + d), dp, ctx).wait_recv()

        def y_copy(self, d):
            w = self.w.at[:, oz, pl.ds(self.piece, 16)]
            return remote(w, w, self.sem(wsend, 9 + d), self.sem(wrecv, 6 + d), dp, y_peer(d))

        def y_start(self):
            for d in range(1, 4):
                self.y_copy(d).start()

        def y_recv(self):
            for d in range(1, 4):
                w = self.w.at[:, oz, pl.ds(64 * k + 16 * ((y + 4 - d) % 4), 16)]
                remote(w, w, self.sem(wsend, 0), self.sem(wrecv, 6 + d), dp, ctx).wait_recv()

        def sib_copy(self, half, n):
            w = self.w.at[:, half, pl.ds(lane, 64)]
            return remote(w, w, self.sem(wsend, 13 + n), self.sem(wrecv, 10 + n), dp, sib_ctx)

        def sib_recv(self, half, n):
            w = self.w.at[:, half, pl.ds(64 - lane, 64)]
            remote(w, w, self.sem(wsend, 0), self.sem(wrecv, 10 + n), dp, ctx).wait_recv()

        def finish(self):
            @pl.when(c == 0)
            def _():
                for j in range(4, 8):
                    self.z_copy(j).wait_send()

            @pl.when(c == 7)
            def _():
                for j in range(4):
                    self.z_copy(j).wait_send()

            for d in range(1, 4):
                self.own_copy(d).wait_send()
                self.other_copy(d).wait_send()
                self.y_copy(d).wait_send()
            self.sib_copy(zh, 0).wait_send()
            self.sib_copy(oz, 1).wait_send()

    gkv, gq, go = Gather(0), Gather(1), Gather(2)
    gkv.z_start()
    gkv.own_start()
    gkv.z_recv()
    gkv.other_start()
    gkv.own_recv()
    locals_[3].wait()
    gkv.sib_copy(zh, 0).start()
    gkv.other_recv()
    gkv.y_start()
    gq.z_start()
    gq.own_start()

    locals_[0].wait()

    def hid_half(half):
        parts = [hid[:, pl.ds(pl.multiple_of((2 * i + half) * 128, 128), 128)] for i in range(4)]
        return jnp.concatenate(parts, axis=1)

    gkv.sib_recv(zh, 0)
    kv_own = jnp.dot(hid_half(zh), wkv[:, zh].reshape(512, 512), preferred_element_type=F32)
    acc_ref[0:4] = jnp.concatenate([kv_own[:, :256], kv_own[:, 256:]], axis=0).reshape(4, 128, 256)

    gkv.y_recv()
    gkv.sib_copy(oz, 1).start()

    for copy in small:
        copy.wait()
    length = len_ref[dp * 4 + y]
    locals_[1].wait()
    locals_[2].wait()
    slot_row = lax.broadcasted_iota(jnp.int32, (4, 2048), 0) == y
    own_q = jnp.sum(jnp.where(slot_row, tq_ref[...].astype(F32), 0.0), axis=0, keepdims=True)
    head_of = lax.broadcasted_iota(jnp.int32, (T_HEADS, 2048), 1) // HD
    diagonal = head_of == lax.broadcasted_iota(jnp.int32, (T_HEADS, 2048), 0)
    q_heads = jnp.where(diagonal, own_q, 0.0).astype(BF16)
    ts = lax.dot_general(q_heads, tk[...], (((1,), (1,)), ((), ())), preferred_element_type=F32) * SCALE
    t_valid = pos * ROWS + lax.broadcasted_iota(jnp.int32, (T_HEADS, ROWS), 1) < length
    ts = jnp.where(t_valid, ts, BIG)
    t_best = jnp.max(ts, axis=1, keepdims=True)
    t_weights = jnp.where(t_valid, jnp.exp(ts - t_best), 0.0)
    t_total = jnp.sum(t_weights, axis=1, keepdims=True)
    t_out = jnp.dot(t_weights.astype(BF16), tv[...], preferred_element_type=F32)
    t_sum = jnp.sum(jnp.where(diagonal, t_out * thead_ref[...], 0.0), axis=1, keepdims=True)
    eye = lax.broadcasted_iota(jnp.int32, (T_HEADS, 128), 0) == lax.broadcasted_iota(jnp.int32, (T_HEADS, 128), 1)

    def row_of(column):
        return jnp.sum(jnp.where(eye, column, 0.0), axis=0, keepdims=True)

    tbuf[pos] = jnp.concatenate([row_of(t_best), row_of(t_total), row_of(t_sum)], axis=1)

    def t_copy(d):
        return remote(tbuf.at[pos], tbuf.at[pos], t_send.at[d], t_recv.at[d], dp, line + (pos + d) % 16)

    for d in range(1, 16):
        t_copy(d).start()

    gkv.sib_recv(oz, 1)
    kv_all = jnp.dot(hid_half(oz), wkv[:, oz].reshape(512, 512), preferred_element_type=F32)
    kv_first = acc_ref[0:4].reshape(512, 256)
    keys = (kv_all[:, :256] + kv_first[:256]).astype(BF16)
    own = 2 * c + k
    for h in range(KV_HEADS):
        kvb[own, 0, h] = keys[:, h * HD : (h + 1) * HD]

    def ring_copy(b, j):
        ref = kvb.at[2 * b + k, j]
        return remote(ref, ref, kv_send.at[b, j], kv_recv.at[2 * b + k, j], dp, ctx + 2)

    def back_copy(b, j):
        ref = kvb.at[2 * b + k, j]
        return remote(ref, ref, kv_send.at[b, j], kv_recv.at[2 * b + k, j], dp, ctx - 2)

    def sib_copy(b, j):
        ref = kvb.at[2 * b + k, j]
        return remote(ref, ref, sib_send.at[b, j], kv_recv.at[2 * b + k, j], dp, sib_ctx)

    def kv_wait(block, j):
        ref = kvb.at[block, j]
        remote(ref, ref, kv_send.at[0, 0], kv_recv.at[block, j], dp, ctx).wait_recv()

    def send_own(j):
        @pl.when(c < 7)
        def _():
            ring_copy(c, j).start()

        sib_copy(c, j).start()

    send_own(0)
    values = (kv_all[:, 256:] + kv_first[256:]).astype(BF16)
    for h in range(KV_HEADS):
        for part in range(2):
            block = values[part * 128 : (part + 1) * 128, h * HD : (h + 1) * HD]
            kvb[own, 1, h, pl.ds(part * 128, 128)] = block.T
    send_own(1)

    gq.z_recv()
    gq.other_start()
    gq.own_recv()
    locals_[4].wait()
    gq.sib_copy(zh, 0).start()
    go.z_start()
    go.own_start()
    gq.other_recv()
    gq.y_start()

    def attend(b, diag):
        for h in range(KV_HEADS):
            kp = jnp.concatenate([kvb[2 * b, 0, h], kvb[2 * b + 1, 0, h]], axis=0)
            v0, v1 = kvb[2 * b, 1, h], kvb[2 * b + 1, 1, h]
            vt = jnp.concatenate([v0[:128], v0[128:], v1[:128], v1[128:]], axis=1)
            for g in range(GROUPS):
                i = h * GROUPS + g
                s = jnp.dot(kp, qt[h, :, g * ROWS : (g + 1) * ROWS], preferred_element_type=F32) * (SCALE * LOG2E)
                if diag:
                    key = lax.broadcasted_iota(jnp.int32, (2 * ROWS, ROWS), 0)
                    row = lax.broadcasted_iota(jnp.int32, (2 * ROWS, ROWS), 1)
                    s = jnp.where(key <= k * ROWS + row, s, BIG)
                best = jnp.max(s, axis=0, keepdims=True)
                if not diag:
                    old = m_ref[i : i + 1, :]
                    best = jnp.maximum(old, best)
                    carry = jnp.exp2(old - best)
                p = jnp.exp2(s - best)
                total = jnp.sum(p, axis=0, keepdims=True)
                out = jnp.dot(vt, p.astype(BF16), preferred_element_type=F32)
                m_ref[i : i + 1, :] = best
                if diag:
                    l_ref[i : i + 1, :] = total
                    acc_ref[i] = out
                else:
                    l_ref[i : i + 1, :] = l_ref[i : i + 1, :] * carry + total
                    acc_ref[i] = acc_ref[i] * carry + out

    def forward(b):
        for j in range(2):
            kv_wait(2 * b + k, j)

            @pl.when(c < 7)
            def _():
                ring_copy(b, j).start()

            sib_copy(b, j).start()

    @pl.when(c >= 1)
    def _():
        forward(c - 1)

    gq.y_recv()
    gq.sib_copy(oz, 1).start()
    go.z_recv()
    go.other_start()
    gq.sib_recv(zh, 0)
    gq.sib_recv(oz, 1)
    query = jnp.dot(hid[...], wq[...].reshape(D, HEADS * HD), preferred_element_type=F32).astype(BF16)
    for i in range(HEADS):
        qt[i // GROUPS, :, (i % GROUPS) * ROWS : (i % GROUPS + 1) * ROWS] = query[:, i * HD : (i + 1) * HD].T
    go.own_recv()
    locals_[5].wait()
    go.sib_copy(zh, 0).start()
    for j in range(2):
        kv_wait(2 * c + 1 - k, j)
    attend(c, True)
    go.other_recv()
    go.y_start()

    def step(s, carry):
        @pl.when(s <= c)
        def _():
            forward(c - s)

        @pl.when(s == 2)
        def _():
            go.y_recv()
            go.sib_copy(oz, 1).start()

        @pl.when(s - 1 <= c)
        def _():
            b = c - s + 1
            for j in range(2):
                kv_wait(2 * b + 1 - k, j)
            attend(b, False)

        return carry

    lax.fori_loop(2, 9, step, 0)

    for i in range(HEADS):
        att[:, i * HD : (i + 1) * HD] = (acc_ref[i] / l_ref[i : i + 1, :]).astype(BF16).T
    go.sib_recv(zh, 0)
    go.sib_recv(oz, 1)
    hidden = hid[...].astype(F32) + jnp.dot(att[...], wo[...].reshape(D, D), preferred_element_type=F32)
    valid = pos * ROWS + lax.broadcasted_iota(jnp.int32, (ROWS, 1), 0) < length
    rate = jnp.where(valid, lax.rsqrt(jnp.mean(hidden * hidden, axis=1, keepdims=True) + 1e-05), 0.0)
    part = jnp.sum(hidden * rate, axis=0, keepdims=True) * gain_ref[...]
    out_ref[...] = jnp.where(valid, hidden, 0.0)

    def chain_copy():
        return remote(cstage, chain, c_send, c_recv, dp, ctx + 2)

    @pl.when(c == 0)
    def _():
        chain[...] = jnp.zeros_like(chain)

    @pl.when(jnp.logical_and(c >= 1, c <= 6))
    def _():
        remote(chain, chain, c_send, c_recv, dp, ctx).wait_recv()

    @pl.when(c <= 5)
    def _():
        cstage[...] = part + chain[...]
        chain_copy().start()

    def p_copy(r, d):
        return remote(pbuf.at[r], pbuf.at[r], p_send.at[d], p_recv.at[r], dp, line + (pos + d) % 16)

    root = 2 * (c - 6) + k

    @pl.when(c == 6)
    def _():
        pbuf[root] = part + chain[...]

    @pl.when(c == 7)
    def _():
        pbuf[root] = part

    @pl.when(c >= 6)
    def _():
        for d in range(1, 16):
            p_copy(root, d).start()

    for d in range(1, 16):
        ref = tbuf.at[(pos + 16 - d) % 16]
        remote(ref, ref, t_send.at[0], t_recv.at[d], dp, ctx).wait_recv()
    stats = jnp.concatenate([tbuf[i] for i in range(16)], axis=0)
    bests = stats[:, :128]
    factor = jnp.exp(bests - jnp.max(bests, axis=0, keepdims=True))
    total = jnp.sum(stats[:, 128:256] * factor, axis=0, keepdims=True)
    above = jnp.sum(stats[:, 256:] * factor, axis=0, keepdims=True)
    in_heads = lax.broadcasted_iota(jnp.int32, (1, 128), 1) < T_HEADS
    t_score = jnp.sum(jnp.where(in_heads, above / jnp.where(in_heads, total, 1.0), 0.0), axis=1, keepdims=True)

    for r in range(4):
        @pl.when(pos != 12 + r)
        def _():
            ref = pbuf.at[r]
            remote(ref, ref, c_send, p_recv.at[r], dp, ctx).wait_recv()

    pooled_sum = (pbuf[0] + pbuf[1]) + (pbuf[2] + pbuf[3])
    pooled = pooled_sum / length.astype(F32)
    ybuf[y] = jnp.concatenate([pooled, jnp.broadcast_to(t_score, (1, 128))], axis=1)

    def y_copy(d):
        return remote(ybuf.at[y], ybuf.at[y], y_send.at[d], y_recv.at[d], dp, y_peer(d))

    for d in range(1, 4):
        y_copy(d).start()
    for d in range(1, 4):
        ref = ybuf.at[(y + 4 - d) % 4]
        remote(ref, ref, y_send.at[0], y_recv.at[d], dp, ctx).wait_recv()

    lanes = lax.broadcasted_iota(jnp.int32, (1, 128), 1)
    scores = jnp.zeros((1, 128), F32)
    t_row = jnp.zeros((1, 128), F32)
    for i in range(4):
        row = ybuf[i]
        student = jnp.sum(row[:, :D] * shead_ref[...], axis=1, keepdims=True)
        scores = scores + jnp.where(lanes == dp * 4 + i, student, 0.0)
        scores = scores + jnp.where(lanes == 64 + dp * 4 + i, row[:, D:], 0.0)
        t_row = t_row + jnp.where(lanes == i, row[:, D:], 0.0)
        pooled_ref[i : i + 1, :] = row[:, :D]
    tscore_ref[...] = t_row
    dbuf[dp] = scores

    def d_copy(d):
        return remote(dbuf.at[dp], dbuf.at[dp], d_send.at[d], d_recv.at[d], (dp + d) % 8, ctx)

    for d in range(1, 8):
        d_copy(d).start()

    @pl.when(c < 7)
    def _():
        def sent(s, carry):
            for j in range(2):
                ring_copy(s, j).wait_send()
            return carry

        lax.fori_loop(0, c + 1, sent, 0)

    def sib_sent(s, carry):
        for j in range(2):
            sib_copy(s, j).wait_send()
        return carry

    lax.fori_loop(0, c + 1, sib_sent, 0)
    for gather in (gkv, gq, go):
        gather.finish()
    for d in range(1, 16):
        t_copy(d).wait_send()

    @pl.when(c <= 5)
    def _():
        chain_copy().wait_send()

    @pl.when(c >= 6)
    def _():
        for d in range(1, 16):
            p_copy(root, d).wait_send()

    for d in range(1, 4):
        y_copy(d).wait_send()

    for d in range(1, 8):
        ref = dbuf.at[(dp + 8 - d) % 8]
        remote(ref, ref, d_send.at[0], d_recv.at[d], dp, ctx).wait_recv()
    every = dbuf[0]
    for i in range(1, 8):
        every = every + dbuf[i]

    threads = list_ref.shape[1]
    student_all, teacher_all = every[:, :threads], every[:, 64 : 64 + threads]
    target = teacher_all + rel_ref[...].astype(F32)
    member = lax.broadcasted_iota(jnp.int32, (8, threads), 0) == list_ref[...]

    def log_soft(logits):
        masked = jnp.where(member, logits, BIG)
        top = jnp.max(masked, axis=1, keepdims=True)
        shifted = jnp.where(member, jnp.exp(masked - top), 0.0)
        return masked - top - jnp.log(jnp.sum(shifted, axis=1, keepdims=True))

    target_log = log_soft(target)
    student_log = log_soft(student_all)
    target_prob = jnp.where(member, jnp.exp(target_log), 0.0)
    terms = jnp.where(member, target_prob * (target_log - student_log), 0.0)
    div_ref[...] = jnp.broadcast_to(jnp.sum(terms, axis=1, keepdims=True), (8, 128))

    for d in range(1, 8):
        d_copy(d).wait_send()


def local(
    student_hidden, w_query, w_keyval, w_out, norm_gain, student_head, teacher_query, teacher_keys, teacher_values,
    teacher_head, thread_lengths, list_index, relevance,
):
    vmem = pl.BlockSpec(memory_space=pltpu.VMEM)
    anywhere = pl.BlockSpec(memory_space=pl.ANY)
    dma = pltpu.SemaphoreType.DMA
    out, pooled, tscore, div = pl.pallas_call(
        kernel,
        out_shape=(
            jax.ShapeDtypeStruct((ROWS, D), F32),
            jax.ShapeDtypeStruct((4, D), F32),
            jax.ShapeDtypeStruct((1, 128), F32),
            jax.ShapeDtypeStruct((8, 128), F32),
        ),
        in_specs=[anywhere] * 13,
        out_specs=(vmem,) * 4,
        scratch_shapes=[
            pltpu.VMEM((ROWS, D), BF16),
            pltpu.VMEM((4, 2, 128, 512), BF16),
            pltpu.VMEM((4, 2, 128, D), BF16),
            pltpu.VMEM((4, 2, 128, D), BF16),
            pltpu.VMEM((ROWS, 2048), BF16),
            pltpu.VMEM((ROWS, 2048), BF16),
            pltpu.VMEM((16, 2, KV_HEADS, 256, 128), BF16),
            pltpu.VMEM((2, 2, KV_HEADS, 256, 128), BF16),
            pltpu.VMEM((KV_HEADS, HD, GROUPS * ROWS), BF16),
            pltpu.VMEM((ROWS, D), BF16),
            pltpu.VMEM((HEADS, ROWS), F32),
            pltpu.VMEM((HEADS, ROWS), F32),
            pltpu.VMEM((HEADS, HD, ROWS), F32),
            pltpu.VMEM((16, 1, 384), F32),
            pltpu.VMEM((1, D), F32),
            pltpu.VMEM((1, D), F32),
            pltpu.VMEM((4, 1, D), F32),
            pltpu.VMEM((4, 1, D + 128), F32),
            pltpu.VMEM((8, 1, 128), F32),
            pltpu.VMEM((1, D), F32),
            pltpu.VMEM((1, D), F32),
            pltpu.VMEM((4, 2048), BF16),
            pltpu.VMEM((1, 2048), F32),
            pltpu.SMEM((32,), jnp.int32),
            pltpu.VMEM((1, 32), jnp.int32),
            pltpu.VMEM((1, 32), jnp.int32),
            dma((13,)),
            dma((3, 15)),
            dma((3, 12)),
            dma((16, 2)),
            dma((8, 2)),
            dma((8, 2)),
            dma((2,)),
            dma((2, 2)),
            dma((2, 2)),
            dma((16,)),
            dma((16,)),
            dma,
            dma,
            dma((16,)),
            dma((4,)),
            dma((4,)),
            dma((4,)),
            dma((8,)),
            dma((8,)),
        ],
        compiler_params=pltpu.CompilerParams(
            collective_id=0, has_side_effects=True, vmem_limit_bytes=60 * 1024 * 1024
        ),
        cost_estimate=pl.CostEstimate(flops=10**10, bytes_accessed=8 * 2**20, transcendentals=8 * 10**6),
    )(
        student_hidden, w_keyval, w_query, w_out, norm_gain.reshape(1, -1), student_head.reshape(1, -1), teacher_query,
        teacher_keys, teacher_values, teacher_head.reshape(1, -1), thread_lengths, list_index.reshape(1, -1),
        relevance.reshape(1, -1),
    )
    return out, pooled, tscore[0, :4], div[:, 0]


def solution(mesh):
    return jax.shard_map(
        local,
        mesh=mesh,
        in_specs=(
            P(("dp", "ctx"), None), P("dp", None), P("dp", None), P("dp", None), P(), P(), P("dp", None),
            P(("dp", "ctx"), None), P(("dp", "ctx"), None), P(), P(), P(), P(),
        ),
        out_specs=(P(("dp", "ctx"), None), P("dp", None), P("dp"), P()),
        check_vma=False,
    )
```

```python
import functools

import jax
import jax.numpy as jnp
from jax import lax
from jax.experimental import pallas as pl
from jax.experimental.pallas import tpu as pltpu
from jax.sharding import PartitionSpec as P

HEADS = 8
KV_HEADS = 2
GROUPS = 4
HD = 128
T_HEADS = 16
ROWS = 256
D = 1024
CHIPS = 8
BIG = -1e30
F32 = jnp.float32
BF16 = jnp.bfloat16
SCALE = HD ** (-0.5)
LOG2E = 1.4426950408889634
MESH = pl.DeviceIdType.MESH


def kernel(
    hid_in, wkv_in, wq_in, wo_in, gain_in, shead_in, tq_in, tk_in, tv_in, thead_in, len_in, list_in, rel_in,
    out_ref, pooled_ref, tscore_ref, div_ref,
    hid, wkv, wq, wo, tk, tv, kvb, relay, qt, att, m_ref, l_ref, acc_ref,
    tbuf, chain, cstage, pbuf, ybuf, sbuf, kv_part,
    gain_ref, shead_ref, tq_ref, thead_ref, len_ref, list_ref, rel_ref,
    lsem, wsend, wrecv, kv_recv, kv_send, sib_send, rev_send, relay_recv, relay_send,
    t_send, t_recv, c_send, c_recv, p_send, p_recv, y_send, y_recv, s_send, s_recv,
):
    dp = lax.axis_index("dp")
    ctx = lax.axis_index("ctx")
    x, zh = dp // 2, dp % 2
    y, pos = ctx // 16, ctx % 16
    c, k = pos // 2, pos % 2
    oz = 1 - zh
    other_dp = 2 * x + oz
    sib_ctx = ctx + 1 - 2 * k
    line = y * 16

    def remote(src, dst, ssem, rsem, to_dp, to_ctx):
        return pltpu.make_async_remote_copy(
            src_ref=src, dst_ref=dst, send_sem=ssem, recv_sem=rsem, device_id=(to_dp, to_ctx), device_id_type=MESH
        )

    def x_peer(d):
        return 2 * ((x + d) % 4) + zh

    def y_peer(d):
        return ((y + d) % 4) * 16 + pos

    thread = dp * 4 + y

    def team(d):
        there = (thread + d) % 32
        return there // 4, (there % 4) * 16 + pos

    lane = 64 * k
    locals_ = [
        pltpu.make_async_copy(hid_in, hid, lsem.at[0]),
        pltpu.make_async_copy(tk_in, tk, lsem.at[1]),
        pltpu.make_async_copy(tv_in, tv, lsem.at[2]),
    ]
    weights = [(wkv_in, wkv), (wq_in, wq), (wo_in, wo)]
    for i, (w_in, w) in enumerate(weights):
        locals_.append(
            pltpu.make_async_copy(w_in.at[pl.ds(lane, 64)], w.at[x, zh, pl.ds(lane, 64)], lsem.at[3 + i])
        )
    small = [
        (gain_in, gain_ref), (shead_in, shead_ref), (tq_in, tq_ref), (thead_in, thead_ref), (len_in, len_ref),
        (list_in, list_ref), (rel_in, rel_ref),
    ]
    small = [pltpu.make_async_copy(src, dst, lsem.at[6 + i]) for i, (src, dst) in enumerate(small)]
    for copy in (locals_[0], locals_[3], locals_[1], locals_[2], locals_[4], locals_[5]):
        copy.start()
    for copy in small:
        copy.start()

    barrier = pltpu.get_barrier_semaphore()

    def greet(to_dp, to_ctx):
        pl.semaphore_signal(barrier, inc=1, device_id=(to_dp, to_ctx), device_id_type=MESH)

    for d in range(1, 16):
        greet(dp, line + (pos + d) % 16)
    for d in range(1, 32):
        greet(*team(d))

    @pl.when(c == 0)
    def _():
        for j in range(4, 8):
            greet(other_dp, line + 2 * j + k)

    @pl.when(c == 7)
    def _():
        for j in range(5):
            greet(other_dp, line + 2 * j + k)

    @pl.when(jnp.logical_and(c >= 1, c <= 4))
    def _():
        greet(other_dp, line + 14 + k)

    @pl.when(jnp.logical_and(c >= 4, c <= 6))
    def _():
        greet(other_dp, line + k)

    @pl.when(c == 1)
    def _():
        greet(other_dp, line + 8 + k)

    @pl.when(c == 4)
    def _():
        greet(other_dp, line + 2 + k)

    def least(value, n):
        return (value + 8 - n) // 8

    more = 3 - 2 * least(c, 1) - least(c, 2) + 2 * least(c, 4) - 2 * least(c, 5) + 4 * least(c, 7)
    pl.semaphore_wait(barrier, 47 + more)

    class Gather:
        def __init__(self, i):
            self.i = i
            self.w_in, self.w = weights[i]
            self.piece = 64 * k + 16 * y

        def sem(self, table, n):
            return table.at[self.i, n]

        def z_copy(self, j):
            w = self.w.at[x, zh, pl.ds(self.piece, 16)]
            return remote(
                self.w_in.at[pl.ds(self.piece, 16)], w, self.sem(wsend, j % 4), self.sem(wrecv, 0),
                other_dp, line + 2 * j + k,
            )

        def z_start(self):
            @pl.when(c == 0)
            def _():
                for j in range(4, 8):
                    self.z_copy(j).start()

            @pl.when(c == 7)
            def _():
                for j in range(4):
                    self.z_copy(j).start()

        def z_recv(self):
            w = self.w.at[x, oz, pl.ds(self.piece, 16)]
            remote(w, w, self.sem(wsend, 0), self.sem(wrecv, 0), other_dp, ctx).wait_recv()

        def own_copy(self, d):
            return remote(
                self.w_in.at[pl.ds(lane, 64)], self.w.at[x, zh, pl.ds(lane, 64)],
                self.sem(wsend, 3 + d), self.sem(wrecv, d), x_peer(d), ctx,
            )

        def own_start(self):
            for d in range(1, 4):
                self.own_copy(d).start()

        def own_recv(self):
            for d in range(1, 4):
                w = self.w.at[(x + 4 - d) % 4, zh, pl.ds(lane, 64)]
                remote(w, w, self.sem(wsend, 0), self.sem(wrecv, d), dp, ctx).wait_recv()

        def other_copy(self, d):
            w = self.w.at[x, oz, pl.ds(self.piece, 16)]
            return remote(w, w, self.sem(wsend, 6 + d), self.sem(wrecv, 3 + d), x_peer(d), ctx)

        def other_start(self):
            for d in range(1, 4):
                self.other_copy(d).start()

        def other_recv(self):
            for d in range(1, 4):
                w = self.w.at[(x + 4 - d) % 4, oz, pl.ds(self.piece, 16)]
                remote(w, w, self.sem(wsend, 0), self.sem(wrecv, 3 + d), dp, ctx).wait_recv()

        def y_copy(self, d):
            w = self.w.at[:, oz, pl.ds(self.piece, 16)]
            return remote(w, w, self.sem(wsend, 9 + d), self.sem(wrecv, 6 + d), dp, y_peer(d))

        def y_start(self):
            for d in range(1, 4):
                self.y_copy(d).start()

        def y_recv(self):
            for d in range(1, 4):
                w = self.w.at[:, oz, pl.ds(64 * k + 16 * ((y + 4 - d) % 4), 16)]
                remote(w, w, self.sem(wsend, 0), self.sem(wrecv, 6 + d), dp, ctx).wait_recv()

        def sib_copy(self, half, n):
            w = self.w.at[:, half, pl.ds(lane, 64)]
            return remote(w, w, self.sem(wsend, 13 + n), self.sem(wrecv, 10 + n), dp, sib_ctx)

        def sib_recv(self, half, n):
            w = self.w.at[:, half, pl.ds(64 - lane, 64)]
            remote(w, w, self.sem(wsend, 0), self.sem(wrecv, 10 + n), dp, ctx).wait_recv()

        def finish(self):
            @pl.when(c == 0)
            def _():
                for j in range(4, 8):
                    self.z_copy(j).wait_send()

            @pl.when(c == 7)
            def _():
                for j in range(4):
                    self.z_copy(j).wait_send()

            for d in range(1, 4):
                self.own_copy(d).wait_send()
                self.other_copy(d).wait_send()
                self.y_copy(d).wait_send()
            self.sib_copy(zh, 0).wait_send()
            self.sib_copy(oz, 1).wait_send()

    gkv, gq, go = Gather(0), Gather(1), Gather(2)
    gkv.z_start()
    gkv.own_start()

    for copy in small:
        copy.wait()
    length = len_ref[thread]
    slot_row = lax.broadcasted_iota(jnp.int32, (4, 2048), 0) == y
    own_q = jnp.sum(jnp.where(slot_row, tq_ref[...].astype(F32), 0.0), axis=0, keepdims=True)
    head_of = lax.broadcasted_iota(jnp.int32, (T_HEADS, 2048), 1) // HD
    diagonal = head_of == lax.broadcasted_iota(jnp.int32, (T_HEADS, 2048), 0)
    q_heads = jnp.where(diagonal, own_q, 0.0).astype(BF16)
    locals_[1].wait()
    ts = lax.dot_general(q_heads, tk[...], (((1,), (1,)), ((), ())), preferred_element_type=F32) * SCALE
    t_valid = pos * ROWS + lax.broadcasted_iota(jnp.int32, (T_HEADS, ROWS), 1) < length
    ts = jnp.where(t_valid, ts, BIG)
    t_best = jnp.max(ts, axis=1, keepdims=True)
    t_weights = jnp.where(t_valid, jnp.exp(ts - t_best), 0.0)
    t_total = jnp.sum(t_weights, axis=1, keepdims=True)
    locals_[2].wait()
    t_out = jnp.dot(t_weights.astype(BF16), tv[...], preferred_element_type=F32)
    t_sum = jnp.sum(jnp.where(diagonal, t_out * thead_ref[...], 0.0), axis=1, keepdims=True)
    eye = lax.broadcasted_iota(jnp.int32, (T_HEADS, 128), 0) == lax.broadcasted_iota(jnp.int32, (T_HEADS, 128), 1)

    def row_of(column):
        return jnp.sum(jnp.where(eye, column, 0.0), axis=0, keepdims=True)

    tbuf[pos] = jnp.concatenate([row_of(t_best), row_of(t_total), row_of(t_sum)], axis=1)

    def t_copy(d):
        return remote(tbuf.at[pos], tbuf.at[pos], t_send.at[d], t_recv.at[d], dp, line + (pos + d) % 16)

    gkv.z_recv()
    gkv.other_start()
    gq.z_start()
    gkv.own_recv()
    locals_[3].wait()
    gkv.sib_copy(zh, 0).start()
    gq.own_start()
    gkv.other_recv()
    gkv.y_start()
    for d in range(1, 16):
        t_copy(d).start()
    locals_[0].wait()

    def hid_half(half):
        parts = [hid[:, pl.ds(pl.multiple_of((2 * i + half) * 128, 128), 128)] for i in range(4)]
        return jnp.concatenate(parts, axis=1)

    gkv.sib_recv(zh, 0)
    kv_part[...] = jnp.dot(hid_half(zh), wkv[:, zh].reshape(512, 512), preferred_element_type=F32)
    gkv.y_recv()
    gkv.sib_copy(oz, 1).start()
    gq.z_recv()
    gq.other_start()
    gkv.sib_recv(oz, 1)
    keyval = kv_part[...] + jnp.dot(hid_half(oz), wkv[:, oz].reshape(512, 512), preferred_element_type=F32)
    keyval = keyval.astype(BF16)
    own = 2 * c + k

    def hand(b, q, ssem, to_ctx):
        ref = kvb.at[2 * b + k, q]
        return remote(ref, ref, ssem.at[b, q], kv_recv.at[2 * b + k, q], dp, to_ctx)

    def ring_copy(b, q):
        return hand(b, q, kv_send, ctx + 2)

    def back_copy(b, q):
        return hand(b, q, kv_send, ctx - 2)

    def sib_copy(b, q):
        return hand(b, q, sib_send, sib_ctx)

    def kv_wait(block, q):
        ref = kvb.at[block, q]
        remote(ref, ref, kv_send.at[0, 0], kv_recv.at[block, q], dp, ctx).wait_recv()

    def rev_copy(q):
        return remote(
            kvb.at[own, q], relay.at[c, q], rev_send.at[q], relay_recv.at[c, q], other_dp, line + 8 + k
        )

    def relay_copy(r, q):
        return remote(
            relay.at[r, q], kvb.at[2 * r + k, q], relay_send.at[r, q], kv_recv.at[2 * r + k, q], other_dp, line + 14 + k
        )

    def passes_on(b):
        gap = jnp.logical_or(jnp.logical_and(b == 0, c >= 5), jnp.logical_and(b == 1, c >= 6))
        return jnp.logical_and(c < 7, jnp.logical_not(gap))

    for h in range(KV_HEADS):
        kvb[own, 2 * h] = keyval[:, h * HD : (h + 1) * HD]
        for part in range(2):
            value = keyval[part * 128 : (part + 1) * 128, (KV_HEADS + h) * HD : (KV_HEADS + h + 1) * HD]
            kvb[own, 2 * h + 1, pl.ds(part * 128, 128)] = value.T
        for q in (2 * h, 2 * h + 1):

            @pl.when(c < 7)
            def _():
                ring_copy(c, q).start()

            @pl.when(c == 0)
            def _():
                rev_copy(q).start()

            sib_copy(c, q).start()

    def block_at(s):
        last = -4 * least(s, 3) + 5 * least(s, 4) - least(s, 6) + 2 * least(s, 7)
        before = -least(s, 5) + 2 * least(s, 6)
        return c - s + last * least(c, 7) + before * (least(c, 6) - least(c, 7))

    def forward(s, h):
        b = block_at(s)

        @pl.when(s <= c)
        def _():
            for q in (2 * h, 2 * h + 1):
                kv_wait(2 * b + k, q)

                @pl.when(passes_on(b))
                def _():
                    ring_copy(b, q).start()

                @pl.when(jnp.logical_and(c == 7, b == 0))
                def _():
                    back_copy(b, q).start()

                sib_copy(b, q).start()

    def relay_on(r, h):
        @pl.when(c == 4)
        def _():
            for q in (2 * h, 2 * h + 1):
                ref = relay.at[r, q]
                remote(ref, ref, rev_send.at[q], relay_recv.at[r, q], dp, ctx).wait_recv()
                relay_copy(r, q).start()

    def attend(b, h, diag):
        kp = jnp.concatenate([kvb[2 * b, 2 * h], kvb[2 * b + 1, 2 * h]], axis=0)
        v0, v1 = kvb[2 * b, 2 * h + 1], kvb[2 * b + 1, 2 * h + 1]
        vt = jnp.concatenate([v0[:128], v0[128:], v1[:128], v1[128:]], axis=1)

        def score(g):
            return jnp.dot(kp, qt[h, g], preferred_element_type=F32)

        ahead = score(0)
        for g in range(GROUPS):
            i = h * GROUPS + g
            s = ahead * (SCALE * LOG2E)
            if g + 1 < GROUPS:
                ahead = score(g + 1)
            if diag:
                key = lax.broadcasted_iota(jnp.int32, (2 * ROWS, ROWS), 0)
                row = lax.broadcasted_iota(jnp.int32, (2 * ROWS, ROWS), 1)
                s = jnp.where(key <= k * ROWS + row, s, BIG)
            best = jnp.max(s, axis=0, keepdims=True)
            if not diag:
                old = m_ref[i]
                best = jnp.maximum(old, best)
                carry = jnp.exp2(old - best)
            p = jnp.exp2(s - best)
            total = jnp.sum(p, axis=0, keepdims=True)
            out = jnp.dot(vt, p.astype(BF16), preferred_element_type=F32)
            m_ref[i] = best
            if diag:
                l_ref[i] = total
                acc_ref[i] = out
            else:
                l_ref[i] = l_ref[i] * carry + total
                acc_ref[i] = acc_ref[i] * carry + out

    gq.other_recv()
    gq.y_start()
    gq.own_recv()
    locals_[4].wait()
    gq.sib_copy(zh, 0).start()
    go.z_start()
    go.own_start()
    for h in range(KV_HEADS):
        forward(1, h)
        relay_on(0, h)

    @pl.when(c == 1)
    def _():
        for q in range(4):
            rev_copy(q).start()

    gq.y_recv()
    gq.sib_copy(oz, 1).start()
    forward(2, 0)
    go.z_recv()
    go.other_start()
    gq.sib_recv(zh, 0)
    gq.sib_recv(oz, 1)
    query = jnp.dot(hid[...], wq[...].reshape(D, HEADS * HD), preferred_element_type=F32).astype(BF16)
    for i in range(HEADS):
        qt[i // GROUPS, i % GROUPS] = query[:, i * HD : (i + 1) * HD].T
    forward(2, 1)
    for h in range(KV_HEADS):
        for q in (2 * h, 2 * h + 1):
            kv_wait(2 * c + 1 - k, q)
        attend(c, h, True)
    go.own_recv()
    locals_[5].wait()
    go.sib_copy(zh, 0).start()
    go.other_recv()
    go.y_start()

    def first_part(u):
        return u - 1 - (9 - u) * (1 - (u + 7) // 16)

    def part(a, carry):
        pair, h = a // 2, a % 2

        @pl.when(pair <= c)
        def _():
            b = block_at(pair)
            for j in range(2):
                kv_wait(2 * b + 1 - k, 2 * h + j)
            attend(b, h, False)

        return carry

    def step(s, carry):
        for h in range(KV_HEADS):
            forward(s, h)

            @pl.when(s == 3)
            def _():
                relay_on(1, h)

            u = 2 * s + h
            lax.fori_loop(first_part(u), first_part(u + 1), part, 0)

        @pl.when(s == 5)
        def _():
            go.y_recv()
            go.sib_copy(oz, 1).start()

        return carry

    lax.fori_loop(3, 8, step, 0)
    part(15, 0)

    for i in range(HEADS):
        att[:, i * HD : (i + 1) * HD] = (acc_ref[i] / l_ref[i]).astype(BF16).T
    go.sib_recv(zh, 0)
    go.sib_recv(oz, 1)
    hidden = hid[...].astype(F32) + jnp.dot(att[...], wo[...].reshape(D, D), preferred_element_type=F32)
    valid = pos * ROWS + lax.broadcasted_iota(jnp.int32, (ROWS, 1), 0) < length
    rate = jnp.where(valid, lax.rsqrt(jnp.mean(hidden * hidden, axis=1, keepdims=True) + 1e-05), 0.0)
    part = jnp.sum(hidden * rate, axis=0, keepdims=True) * gain_ref[...]
    out_ref[...] = jnp.where(valid, hidden, 0.0)

    def chain_copy():
        return remote(cstage, chain, c_send, c_recv, dp, ctx + 2)

    @pl.when(c == 0)
    def _():
        chain[...] = jnp.zeros_like(chain)

    @pl.when(jnp.logical_and(c >= 1, c <= 5))
    def _():
        remote(chain, chain, c_send, c_recv, dp, ctx).wait_recv()

    @pl.when(c <= 4)
    def _():
        cstage[...] = part + chain[...]
        chain_copy().start()

    def p_copy(r, d):
        return remote(pbuf.at[r], pbuf.at[r], p_send.at[d], p_recv.at[r], dp, line + (pos + d) % 16)

    root = 2 * (c - 5) + k

    @pl.when(c == 5)
    def _():
        pbuf[root] = part + chain[...]

    @pl.when(c >= 6)
    def _():
        pbuf[root] = part

    @pl.when(c >= 5)
    def _():
        for d in range(1, 16):
            p_copy(root, d).start()

    for d in range(1, 16):
        ref = tbuf.at[(pos + 16 - d) % 16]
        remote(ref, ref, t_send.at[0], t_recv.at[d], dp, ctx).wait_recv()
    stats = jnp.concatenate([tbuf[i] for i in range(16)], axis=0)
    bests = stats[:, :128]
    factor = jnp.exp(bests - jnp.max(bests, axis=0, keepdims=True))
    total = jnp.sum(stats[:, 128:256] * factor, axis=0, keepdims=True)
    above = jnp.sum(stats[:, 256:] * factor, axis=0, keepdims=True)
    in_heads = lax.broadcasted_iota(jnp.int32, (1, 128), 1) < T_HEADS
    t_score = jnp.sum(jnp.where(in_heads, above / jnp.where(in_heads, total, 1.0), 0.0), axis=1, keepdims=True)

    for r in range(6):

        @pl.when(pos != 10 + r)
        def _():
            ref = pbuf.at[r]
            remote(ref, ref, c_send, p_recv.at[r], dp, ctx).wait_recv()

    pooled_sum = ((pbuf[0] + pbuf[1]) + (pbuf[2] + pbuf[3])) + (pbuf[4] + pbuf[5])
    pooled = pooled_sum / length.astype(F32)
    ybuf[y] = pooled
    student = jnp.sum(pooled * shead_ref[...], axis=1, keepdims=True)
    lanes = lax.broadcasted_iota(jnp.int32, (1, 128), 1)
    sbuf[thread] = jnp.where(lanes == thread, student, 0.0) + jnp.where(lanes == 64 + thread, t_score, 0.0)

    def s_copy(d):
        return remote(sbuf.at[thread], sbuf.at[thread], s_send.at[d], s_recv.at[d], *team(d))

    def y_copy(d):
        return remote(ybuf.at[y], ybuf.at[y], y_send.at[d], y_recv.at[d], dp, y_peer(d))

    for d in range(1, 32):
        s_copy(d).start()
    for d in range(1, 4):
        y_copy(d).start()

    def sent(b, carry):
        for q in range(4):

            @pl.when(jnp.logical_or(passes_on(b), jnp.logical_and(c == 7, b == 0)))
            def _():
                ring_copy(b, q).wait_send()

            sib_copy(b, q).wait_send()
        return carry

    lax.fori_loop(0, c + 1, sent, 0)

    @pl.when(c <= 1)
    def _():
        for q in range(4):
            rev_copy(q).wait_send()

    @pl.when(c == 4)
    def _():
        for r in range(2):
            for q in range(4):
                relay_copy(r, q).wait_send()

    for gather in (gkv, gq, go):
        gather.finish()
    for d in range(1, 16):
        t_copy(d).wait_send()

    @pl.when(c <= 4)
    def _():
        chain_copy().wait_send()

    @pl.when(c >= 5)
    def _():
        for d in range(1, 16):
            p_copy(root, d).wait_send()

    for d in range(1, 4):
        y_copy(d).wait_send()

    for d in range(1, 4):
        ref = ybuf.at[(y + 4 - d) % 4]
        remote(ref, ref, y_send.at[0], y_recv.at[d], dp, ctx).wait_recv()
    for i in range(4):
        pooled_ref[i : i + 1, :] = ybuf[i]
    for d in range(1, 32):
        ref = sbuf.at[(thread + 32 - d) % 32]
        remote(ref, ref, s_send.at[0], s_recv.at[d], dp, ctx).wait_recv()
    every = jnp.sum(sbuf[...].reshape(32, 128), axis=0, keepdims=True)
    member_t = lax.broadcasted_iota(jnp.int32, (4, 128), 1) == 64 + dp * 4 + lax.broadcasted_iota(jnp.int32, (4, 128), 0)
    t_column = jnp.sum(jnp.where(member_t, every, 0.0), axis=1, keepdims=True)
    eye4 = lax.broadcasted_iota(jnp.int32, (4, 4), 0) == lax.broadcasted_iota(jnp.int32, (4, 4), 1)
    tscore_ref[...] = jnp.sum(jnp.where(eye4, t_column, 0.0), axis=0, keepdims=True)

    threads = list_ref.shape[1]
    student_all, teacher_all = every[:, :threads], every[:, 64 : 64 + threads]
    target = teacher_all + rel_ref[...].astype(F32)
    member = lax.broadcasted_iota(jnp.int32, (8, threads), 0) == list_ref[...]

    def log_soft(logits):
        masked = jnp.where(member, logits, BIG)
        top = jnp.max(masked, axis=1, keepdims=True)
        shifted = jnp.where(member, jnp.exp(masked - top), 0.0)
        return masked - top - jnp.log(jnp.sum(shifted, axis=1, keepdims=True))

    target_log = log_soft(target)
    student_log = log_soft(student_all)
    target_prob = jnp.where(member, jnp.exp(target_log), 0.0)
    terms = jnp.where(member, target_prob * (target_log - student_log), 0.0)
    div_column = jnp.sum(terms, axis=1, keepdims=True)
    eye8 = lax.broadcasted_iota(jnp.int32, (8, 8), 0) == lax.broadcasted_iota(jnp.int32, (8, 8), 1)
    div_ref[...] = jnp.sum(jnp.where(eye8, div_column, 0.0), axis=0, keepdims=True)

    for d in range(1, 32):
        s_copy(d).wait_send()


def place(out, pooled, tscore, div, out_ref, pooled_ref, tscore_ref, div_ref):
    out_ref[...] = out[...]
    pooled_ref[...] = pooled[...]
    tscore_ref[...] = tscore[...]
    div_ref[...] = div[...]


def local(
    student_hidden, w_query, w_keyval, w_out, norm_gain, student_head, teacher_query, teacher_keys, teacher_values,
    teacher_head, thread_lengths, list_index, relevance,
):
    vmem = pl.BlockSpec(memory_space=pltpu.VMEM)
    anywhere = pl.BlockSpec(memory_space=pl.ANY)
    dma = pltpu.SemaphoreType.DMA
    out, pooled, tscore, div = pl.pallas_call(
        kernel,
        out_shape=(
            jax.ShapeDtypeStruct((ROWS, D), F32),
            jax.ShapeDtypeStruct((4, D), F32),
            jax.ShapeDtypeStruct((1, 4), F32),
            jax.ShapeDtypeStruct((1, 8), F32),
        ),
        in_specs=[anywhere] * 13,
        out_specs=(vmem,) * 4,
        scratch_shapes=[
            pltpu.VMEM((ROWS, D), BF16),
            pltpu.VMEM((4, 2, 128, 512), BF16),
            pltpu.VMEM((4, 2, 128, D), BF16),
            pltpu.VMEM((4, 2, 128, D), BF16),
            pltpu.VMEM((ROWS, 2048), BF16),
            pltpu.VMEM((ROWS, 2048), BF16),
            pltpu.VMEM((16, 4, 256, 128), BF16),
            pltpu.VMEM((2, 4, 256, 128), BF16),
            pltpu.VMEM((KV_HEADS, GROUPS, HD, ROWS), BF16),
            pltpu.VMEM((ROWS, D), BF16),
            pltpu.VMEM((HEADS, 1, ROWS), F32),
            pltpu.VMEM((HEADS, 1, ROWS), F32),
            pltpu.VMEM((HEADS, HD, ROWS), F32),
            pltpu.VMEM((16, 1, 384), F32),
            pltpu.VMEM((1, D), F32),
            pltpu.VMEM((1, D), F32),
            pltpu.VMEM((6, 1, D), F32),
            pltpu.VMEM((4, 1, D), F32),
            pltpu.VMEM((32, 1, 128), F32),
            pltpu.VMEM((ROWS, 512), F32),
            pltpu.VMEM((1, D), F32),
            pltpu.VMEM((1, D), F32),
            pltpu.VMEM((4, 2048), BF16),
            pltpu.VMEM((1, 2048), F32),
            pltpu.SMEM((32,), jnp.int32),
            pltpu.VMEM((1, 32), jnp.int32),
            pltpu.VMEM((1, 32), jnp.int32),
            dma((13,)),
            dma((3, 15)),
            dma((3, 12)),
            dma((16, 4)),
            dma((8, 4)),
            dma((8, 4)),
            dma((4,)),
            dma((2, 4)),
            dma((2, 4)),
            dma((16,)),
            dma((16,)),
            dma,
            dma,
            dma((16,)),
            dma((6,)),
            dma((4,)),
            dma((4,)),
            dma((32,)),
            dma((32,)),
        ],
        compiler_params=pltpu.CompilerParams(
            collective_id=0, has_side_effects=True, vmem_limit_bytes=60 * 1024 * 1024
        ),
        cost_estimate=pl.CostEstimate(flops=10**10, bytes_accessed=8 * 2**20, transcendentals=8 * 10**6),
    )(
        student_hidden, w_keyval, w_query, w_out, norm_gain.reshape(1, -1), student_head.reshape(1, -1), teacher_query,
        teacher_keys, teacher_values, teacher_head.reshape(1, -1), thread_lengths, list_index.reshape(1, -1),
        relevance.reshape(1, -1),
    )
    out, pooled, tscore, div = pl.pallas_call(
        place,
        out_shape=tuple(jax.ShapeDtypeStruct(a.shape, a.dtype) for a in (out, pooled, tscore, div)),
        in_specs=[vmem] * 4,
        out_specs=(vmem,) * 4,
        compiler_params=pltpu.CompilerParams(vmem_limit_bytes=60 * 1024 * 1024),
    )(out, pooled, tscore, div)
    return out, pooled, tscore.reshape(4), div.reshape(8)


def solution(mesh):
    return jax.shard_map(
        local,
        mesh=mesh,
        in_specs=(
            P(("dp", "ctx"), None), P("dp", None), P("dp", None), P("dp", None), P(), P(), P("dp", None),
            P(("dp", "ctx"), None), P(("dp", "ctx"), None), P(), P(), P(), P(),
        ),
        out_specs=(P(("dp", "ctx"), None), P("dp", None), P("dp"), P()),
        check_vma=False,
    )
```

```python
import functools

import jax
import jax.numpy as jnp
from jax import lax
from jax.experimental import pallas as pl
from jax.experimental.pallas import tpu as pltpu
from jax.sharding import PartitionSpec as P

HEADS = 8
KV_HEADS = 2
GROUPS = 4
HD = 128
T_HEADS = 16
ROWS = 256
D = 1024
CHIPS = 8
BIG = -1e30
F32 = jnp.float32
BF16 = jnp.bfloat16
SCALE = HD ** (-0.5)
LOG2E = 1.4426950408889634
MESH = pl.DeviceIdType.MESH


def kernel(
    hid_in, wkv_in, wq_in, wo_in, gain_in, shead_in, tq_in, tk_in, tv_in, thead_in, len_in, list_in, rel_in,
    out_ref, pooled_ref, tscore_ref, div_ref,
    hid, wk, wv, wq, wo, tk, tv, kvb, relay, qt, att, m_ref, l_ref, acc_ref,
    tsib, tbuf, trow, cbuf, cstage, pbuf, rbuf, ybuf, sbuf, kv_part,
    gain_ref, shead_ref, tq_ref, thead_ref, len_ref, list_ref, rel_ref,
    lsem, wsend, wrecv, kv_recv, kv_send, sib_send, rev_send, relay_recv, relay_send,
    t_send, t_recv, c_send, c_recv, p_send, p_recv, r_send, r_recv, y_send, y_recv, s_send, s_recv,
):
    dp = lax.axis_index("dp")
    ctx = lax.axis_index("ctx")
    x, zh = dp // 2, dp % 2
    y, pos = ctx // 16, ctx % 16
    c, k = pos // 2, pos % 2
    oz = 1 - zh
    other_dp = 2 * x + oz
    sib_ctx = ctx + 1 - 2 * k
    line = y * 16

    def remote(src, dst, ssem, rsem, to_dp, to_ctx):
        return pltpu.make_async_remote_copy(
            src_ref=src, dst_ref=dst, send_sem=ssem, recv_sem=rsem, device_id=(to_dp, to_ctx), device_id_type=MESH
        )

    def x_peer(d):
        return 2 * ((x + d) % 4) + zh

    def y_peer(d):
        return ((y + d) % 4) * 16 + pos

    thread = dp * 4 + y

    lane = 64 * k
    locals_ = [
        pltpu.make_async_copy(hid_in, hid, lsem.at[0]),
        pltpu.make_async_copy(tk_in, tk, lsem.at[1]),
        pltpu.make_async_copy(tv_in, tv, lsem.at[2]),
    ]
    weights = [(wkv_in.at[:, pl.ds(0, 256)], wk), (wkv_in.at[:, pl.ds(256, 256)], wv), (wq_in, wq), (wo_in, wo)]
    for i, (w_in, w) in enumerate(weights):
        locals_.append(
            pltpu.make_async_copy(w_in.at[pl.ds(lane, 64)], w.at[x, zh, pl.ds(lane, 64)], lsem.at[3 + i])
        )
    small = [
        (gain_in, gain_ref), (shead_in, shead_ref), (tq_in, tq_ref), (thead_in, thead_ref), (len_in, len_ref),
        (list_in, list_ref), (rel_in, rel_ref),
    ]
    small = [pltpu.make_async_copy(src, dst, lsem.at[7 + i]) for i, (src, dst) in enumerate(small)]
    for copy in [locals_[0]] + locals_[3:] + locals_[1:3]:
        copy.start()
    for copy in small:
        copy.start()

    barrier = pltpu.get_barrier_semaphore()

    def greet(to_dp, to_ctx):
        pl.semaphore_signal(barrier, inc=1, device_id=(to_dp, to_ctx), device_id_type=MESH)

    greet(dp, sib_ctx)
    for d in range(1, 4):
        greet(dp, y_peer(d))
        greet(x_peer(d), ctx)

    @pl.when(c < 7)
    def _():
        greet(dp, ctx + 2)

    @pl.when(c > 0)
    def _():
        greet(dp, ctx - 2)

    @pl.when(c == 0)
    def _():
        for j in range(4, 8):
            greet(other_dp, line + 2 * j + k)

    @pl.when(c == 7)
    def _():
        for j in range(5):
            greet(other_dp, line + 2 * j + k)

    @pl.when(jnp.logical_and(c >= 1, c <= 4))
    def _():
        greet(other_dp, line + 14 + k)

    @pl.when(jnp.logical_and(c >= 4, c <= 6))
    def _():
        greet(other_dp, line + k)

    @pl.when(c == 1)
    def _():
        greet(other_dp, line + 8 + k)

    @pl.when(c == 4)
    def _():
        greet(other_dp, line + 2 + k)

    def least(value, n):
        return (value + 8 - n) // 8

    @pl.when(c == 6)
    def _():
        for j in range(5):
            greet(dp, line + 2 * j + k)

    more = 3 - 2 * least(c, 1) - least(c, 2) + 2 * least(c, 4) - 2 * least(c, 5) + 4 * least(c, 7)
    pl.semaphore_wait(barrier, 10 + least(c, 1) - least(c, 5) - least(c, 7) + more)

    class Gather:
        def __init__(self, i):
            self.i = i
            self.w_in, self.w = weights[i]
            self.piece = 64 * k + 16 * y
            self.ring = i >= 2

        def sem(self, table, n):
            return table.at[self.i, n]

        def z_copy(self, j):
            w = self.w.at[x, zh, pl.ds(self.piece, 16)]
            return remote(
                self.w_in.at[pl.ds(self.piece, 16)], w, self.sem(wsend, j % 4), self.sem(wrecv, 0),
                other_dp, line + 2 * j + k,
            )

        def z_start(self):
            @pl.when(c == 0)
            def _():
                for j in range(4, 8):
                    self.z_copy(j).start()

            @pl.when(c == 7)
            def _():
                for j in range(4):
                    self.z_copy(j).start()

        def z_recv(self):
            w = self.w.at[x, oz, pl.ds(self.piece, 16)]
            remote(w, w, self.sem(wsend, 0), self.sem(wrecv, 0), other_dp, ctx).wait_recv()

        def own_part(self, at, first=0, rows=64):
            return self.w.at[(x + at) % 4, zh, pl.ds(lane + first, rows)]

        def own_copies(self):
            src = self.w_in.at[pl.ds(lane, 64)]
            hops = (1, 3) if self.ring else (1, 2, 3)
            return [
                remote(src, self.own_part(0), self.sem(wsend, 3 + d), self.sem(wrecv, d), x_peer(d), ctx) for d in hops
            ]

        def own_relays(self):
            left, right = self.own_part(3, 0, 32), self.own_part(1, 32, 32)
            return [
                remote(left, left, self.sem(wsend, 5), self.sem(wrecv, 2), x_peer(1), ctx),
                remote(right, right, self.sem(wsend, 15), self.sem(wrecv, 12), x_peer(3), ctx),
            ]

        def own_start(self):
            for copy in self.own_copies():
                copy.start()

        def arrived(self, w, n):
            remote(w, w, self.sem(wsend, 0), self.sem(wrecv, n), dp, ctx).wait_recv()

        def own_mid(self):
            relays = self.own_relays()
            self.arrived(self.own_part(3), 1)
            relays[0].start()
            self.arrived(self.own_part(1), 3)
            relays[1].start()

        def own_recv(self):
            if self.ring:
                self.arrived(self.own_part(2, 0, 32), 2)
                self.arrived(self.own_part(2, 32, 32), 12)
            else:
                for d in range(1, 4):
                    self.arrived(self.own_part(4 - d), d)

        def other_copy(self, d):
            w = self.w.at[x, oz, pl.ds(self.piece, 16)]
            return remote(w, w, self.sem(wsend, 6 + d), self.sem(wrecv, 3 + d), x_peer(d), ctx)

        def other_start(self):
            for d in range(1, 4):
                self.other_copy(d).start()

        def other_recv(self):
            for d in range(1, 4):
                w = self.w.at[(x + 4 - d) % 4, oz, pl.ds(self.piece, 16)]
                remote(w, w, self.sem(wsend, 0), self.sem(wrecv, 3 + d), dp, ctx).wait_recv()

        def y_part(self, at, first=0, count=4):
            return self.w.at[pl.ds(first, count), oz, pl.ds(64 * k + 16 * ((y + at) % 4), 16)]

        def y_copies(self):
            src = self.y_part(0)
            hops = (1, 3) if self.ring else (1, 2, 3)
            return [remote(src, src, self.sem(wsend, 9 + d), self.sem(wrecv, 6 + d), dp, y_peer(d)) for d in hops]

        def y_relays(self):
            left, right = self.y_part(3, 0, 2), self.y_part(1, 2, 2)
            return [
                remote(left, left, self.sem(wsend, 11), self.sem(wrecv, 8), dp, y_peer(1)),
                remote(right, right, self.sem(wsend, 16), self.sem(wrecv, 13), dp, y_peer(3)),
            ]

        def y_start(self):
            for copy in self.y_copies():
                copy.start()

        def y_mid(self):
            relays = self.y_relays()
            self.arrived(self.y_part(3), 7)
            relays[0].start()
            self.arrived(self.y_part(1), 9)
            relays[1].start()

        def y_recv(self):
            if self.ring:
                self.arrived(self.y_part(2, 0, 2), 8)
                self.arrived(self.y_part(2, 2, 2), 13)
            else:
                for d in range(1, 4):
                    self.arrived(self.y_part(4 - d), 6 + d)

        def sib_copy(self, half, n):
            w = self.w.at[:, half, pl.ds(lane, 64)]
            return remote(w, w, self.sem(wsend, 13 + n), self.sem(wrecv, 10 + n), dp, sib_ctx)

        def sib_recv(self, half, n):
            w = self.w.at[:, half, pl.ds(64 - lane, 64)]
            remote(w, w, self.sem(wsend, 0), self.sem(wrecv, 10 + n), dp, ctx).wait_recv()

        def finish(self):
            @pl.when(c == 0)
            def _():
                for j in range(4, 8):
                    self.z_copy(j).wait_send()

            @pl.when(c == 7)
            def _():
                for j in range(4):
                    self.z_copy(j).wait_send()

            copies = self.own_copies() + self.y_copies() + [self.other_copy(d) for d in range(1, 4)]
            for copy in copies + (self.own_relays() + self.y_relays() if self.ring else []):
                copy.wait_send()
            self.sib_copy(zh, 0).wait_send()
            self.sib_copy(oz, 1).wait_send()

    for copy in small:
        copy.wait()
    length = len_ref[thread]
    gk, gv, gq, go = (Gather(i) for i in range(4))

    for gather in (gk, gv):
        gather.z_start()
        gather.own_start()
    for gather in (gk, gv):
        gather.z_recv()
        gather.other_start()
    gq.z_start()
    for gather, copy in ((gk, locals_[3]), (gv, locals_[4])):
        gather.own_recv()
        copy.wait()
        gather.sib_copy(zh, 0).start()
    for gather in (gk, gv):
        gather.other_recv()
        gather.y_start()
    gq.own_start()
    locals_[0].wait()

    def project(half, w):
        parts = [hid[:, pl.ds(pl.multiple_of((2 * i + half) * 128, 128), 128)] for i in range(4)]
        return jnp.dot(jnp.concatenate(parts, axis=1), w[:, half].reshape(512, 256), preferred_element_type=F32)

    gk.sib_recv(zh, 0)
    kv_part[0] = project(zh, wk)
    gv.sib_recv(zh, 0)
    kv_part[1] = project(zh, wv)
    for gather in (gk, gv):
        gather.y_recv()
        gather.sib_copy(oz, 1).start()
    gq.z_recv()
    gq.other_start()
    own = 2 * c + k

    def hand(b, q, ssem, to_ctx):
        ref = kvb.at[2 * b + k, q]
        return remote(ref, ref, ssem.at[b, q], kv_recv.at[2 * b + k, q], dp, to_ctx)

    def ring_copy(b, q):
        return hand(b, q, kv_send, ctx + 2)

    def back_copy(b, q):
        return hand(b, q, kv_send, ctx - 2)

    def sib_copy(b, q):
        return hand(b, q, sib_send, sib_ctx)

    def kv_wait(block, q):
        ref = kvb.at[block, q]
        remote(ref, ref, kv_send.at[0, 0], kv_recv.at[block, q], dp, ctx).wait_recv()

    def rev_copy(q):
        return remote(
            kvb.at[own, q], relay.at[c, q], rev_send.at[q], relay_recv.at[c, q], other_dp, line + 8 + k
        )

    def relay_copy(r, q):
        return remote(
            relay.at[r, q], kvb.at[2 * r + k, q], relay_send.at[r, q], kv_recv.at[2 * r + k, q], other_dp, line + 14 + k
        )

    def passes_on(b):
        gap = jnp.logical_or(jnp.logical_and(b == 0, c >= 4), jnp.logical_and(b == 1, c >= 6))
        return jnp.logical_and(c < 7, jnp.logical_not(gap))

    def passes_back(b):
        return jnp.logical_and(b == 0, c >= 6)

    def send_own(q):
        @pl.when(c < 7)
        def _():
            ring_copy(c, q).start()

        @pl.when(c == 0)
        def _():
            rev_copy(q).start()

        sib_copy(c, q).start()

    gk.sib_recv(oz, 1)
    keys = (kv_part[0] + project(oz, wk)).astype(BF16)
    for h in range(KV_HEADS):
        kvb[own, h] = keys[:, h * HD : (h + 1) * HD]
        send_own(h)
    gv.sib_recv(oz, 1)
    values = (kv_part[1] + project(oz, wv)).astype(BF16)
    for h in range(KV_HEADS):
        for part in range(2):
            kvb[own, 2 + h, pl.ds(part * 128, 128)] = values[part * 128 : (part + 1) * 128, h * HD : (h + 1) * HD].T
        send_own(2 + h)

    def block_at(s):
        last = -4 * least(s, 3) + 5 * least(s, 4) - least(s, 6) + 2 * least(s, 7)
        before = -2 * least(s, 4) + 3 * least(s, 5)
        return c - s + last * least(c, 7) + before * (least(c, 6) - least(c, 7))

    def forward(s, j):
        b = block_at(s)

        @pl.when(s <= c)
        def _():
            for q in (2 * j, 2 * j + 1):
                kv_wait(2 * b + k, q)

                @pl.when(passes_on(b))
                def _():
                    ring_copy(b, q).start()

                @pl.when(passes_back(b))
                def _():
                    back_copy(b, q).start()

                sib_copy(b, q).start()

    def relay_on(r, j):
        @pl.when(c == 4)
        def _():
            for q in (2 * j, 2 * j + 1):
                ref = relay.at[r, q]
                remote(ref, ref, rev_send.at[q], relay_recv.at[r, q], dp, ctx).wait_recv()
                relay_copy(r, q).start()

    def attend(b, h, diag):
        kp = jnp.concatenate([kvb[2 * b, h], kvb[2 * b + 1, h]], axis=0)
        v0, v1 = kvb[2 * b, 2 + h], kvb[2 * b + 1, 2 + h]
        vt = jnp.concatenate([v0[:128], v0[128:], v1[:128], v1[128:]], axis=1)
        queries = jnp.concatenate([qt[h, g] for g in range(GROUPS)], axis=1)
        wide = jnp.dot(kp, queries, preferred_element_type=F32) * (SCALE * LOG2E)
        for g in range(GROUPS):
            i = h * GROUPS + g
            s = wide[:, g * ROWS : (g + 1) * ROWS]
            if diag:
                key = lax.broadcasted_iota(jnp.int32, (2 * ROWS, ROWS), 0)
                row = lax.broadcasted_iota(jnp.int32, (2 * ROWS, ROWS), 1)
                s = jnp.where(key <= k * ROWS + row, s, BIG)
            best = jnp.max(s, axis=0, keepdims=True)
            if not diag:
                old = m_ref[i]
                best = jnp.maximum(old, best)
                carry = jnp.exp2(old - best)
            p = jnp.exp2(s - best)
            total = jnp.sum(p, axis=0, keepdims=True)
            out = jnp.dot(vt, p.astype(BF16), preferred_element_type=F32)
            m_ref[i] = best
            if diag:
                l_ref[i] = total
                acc_ref[i] = out
            else:
                l_ref[i] = l_ref[i] * carry + total
                acc_ref[i] = acc_ref[i] * carry + out

    gq.own_mid()
    gq.other_recv()
    gq.y_start()
    go.z_start()
    slot_row = lax.broadcasted_iota(jnp.int32, (4, 2048), 0) == y
    own_q = jnp.sum(jnp.where(slot_row, tq_ref[...].astype(F32), 0.0), axis=0, keepdims=True)
    head_of = lax.broadcasted_iota(jnp.int32, (T_HEADS, 2048), 1) // HD
    diagonal = head_of == lax.broadcasted_iota(jnp.int32, (T_HEADS, 2048), 0)
    q_heads = jnp.where(diagonal, own_q, 0.0).astype(BF16)
    locals_[1].wait()
    ts = lax.dot_general(q_heads, tk[...], (((1,), (1,)), ((), ())), preferred_element_type=F32) * SCALE
    t_valid = pos * ROWS + lax.broadcasted_iota(jnp.int32, (T_HEADS, ROWS), 1) < length
    ts = jnp.where(t_valid, ts, BIG)
    t_best = jnp.max(ts, axis=1, keepdims=True)
    t_weights = jnp.where(t_valid, jnp.exp(ts - t_best), 0.0)
    t_total = jnp.sum(t_weights, axis=1, keepdims=True)
    locals_[2].wait()
    t_out = jnp.dot(t_weights.astype(BF16), tv[...], preferred_element_type=F32)
    t_sum = jnp.sum(jnp.where(diagonal, t_out * thead_ref[...], 0.0), axis=1, keepdims=True)
    eye = lax.broadcasted_iota(jnp.int32, (T_HEADS, 128), 0) == lax.broadcasted_iota(jnp.int32, (T_HEADS, 128), 1)

    def row_of(column):
        return jnp.sum(jnp.where(eye, column, 0.0), axis=0, keepdims=True)

    tsib[k] = jnp.concatenate([row_of(t_best), row_of(t_total), row_of(t_sum)], axis=1)

    def t_copy():
        return remote(tsib.at[k], tsib.at[k], t_send.at[0], t_recv.at[0], dp, sib_ctx)

    def merged(rows):
        best = jnp.max(rows[:, :128], axis=0, keepdims=True)
        factor = jnp.exp(rows[:, :128] - best)
        sums = [jnp.sum(rows[:, n : n + 128] * factor, axis=0, keepdims=True) for n in (128, 256)]
        return jnp.concatenate([best] + sums, axis=1)

    def t_gather():
        return remote(tbuf.at[c], tbuf.at[c], t_send.at[1], t_recv.at[1 + c], dp, line + 12 + k)

    t_copy().start()

    gq.own_recv()
    locals_[5].wait()
    gq.sib_copy(zh, 0).start()
    go.own_start()
    forward(1, 0)
    relay_on(0, 0)
    gq.y_mid()
    forward(1, 1)
    relay_on(0, 1)

    @pl.when(c == 1)
    def _():
        for q in range(4):
            rev_copy(q).start()

    go.z_recv()
    go.other_start()
    gq.y_recv()
    gq.sib_copy(oz, 1).start()
    forward(2, 0)
    gq.sib_recv(zh, 0)
    gq.sib_recv(oz, 1)
    query = jnp.dot(hid[...], wq[...].reshape(D, HEADS * HD), preferred_element_type=F32).astype(BF16)
    for i in range(HEADS):
        qt[i // GROUPS, i % GROUPS] = query[:, i * HD : (i + 1) * HD].T
    forward(2, 1)
    remote(tsib.at[1 - k], tsib.at[1 - k], t_send.at[0], t_recv.at[0], dp, ctx).wait_recv()
    tbuf[c] = merged(jnp.concatenate([tsib[0], tsib[1]], axis=0))

    @pl.when(c != 6)
    def _():
        t_gather().start()

    go.own_mid()
    for h in range(KV_HEADS):
        for q in (h, 2 + h):
            kv_wait(2 * c + 1 - k, q)
        attend(c, h, True)
    go.other_recv()
    go.y_start()

    def first_part(u):
        return u - 1 - (9 - u) * (1 - (u + 7) // 16)

    def part(a, carry):
        pair, h = a // 2, a % 2

        @pl.when(pair <= c)
        def _():
            b = block_at(pair)
            for j in range(2):
                kv_wait(2 * b + 1 - k, 2 * j + h)
            attend(b, h, False)

        return carry

    def step(s, carry):
        for j in range(2):
            forward(s, j)

            @pl.when(s == 3)
            def _():
                relay_on(1, j)

            u = 2 * s + j
            lax.fori_loop(first_part(u), first_part(u + 1), part, 0)

        @pl.when(s == 3)
        def _():
            go.own_recv()
            locals_[6].wait()
            go.sib_copy(zh, 0).start()

        @pl.when(s == 4)
        def _():
            go.y_mid()

        @pl.when(s == 5)
        def _():
            go.y_recv()
            go.sib_copy(oz, 1).start()

        return carry

    lax.fori_loop(3, 8, step, 0)
    part(15, 0)

    for i in range(HEADS):
        att[:, i * HD : (i + 1) * HD] = (acc_ref[i] / l_ref[i]).astype(BF16).T
    go.sib_recv(zh, 0)
    go.sib_recv(oz, 1)
    hidden = hid[...].astype(F32) + jnp.dot(att[...], wo[...].reshape(D, D), preferred_element_type=F32)
    valid = pos * ROWS + lax.broadcasted_iota(jnp.int32, (ROWS, 1), 0) < length
    rate = jnp.where(valid, lax.rsqrt(jnp.mean(hidden * hidden, axis=1, keepdims=True) + 1e-05), 0.0)
    part = jnp.sum(hidden * rate, axis=0, keepdims=True) * gain_ref[...]
    out_ref[...] = jnp.where(valid, hidden, 0.0)

    def chain_copy():
        return remote(cstage, cbuf.at[c], c_send, c_recv.at[c], dp, line + 12 + k)

    cstage[...] = part

    @pl.when(c <= 5)
    def _():
        chain_copy().start()

    root = 2 * (c - 6) + k
    lanes = lax.broadcasted_iota(jnp.int32, (1, 128), 1)

    @pl.when(c == 7)
    def _():
        trow[...] = jnp.zeros_like(trow)

    @pl.when(c == 6)
    def _():
        for i in (0, 1, 2, 3, 4, 5, 7):
            remote(tbuf.at[i], tbuf.at[i], t_send.at[0], t_recv.at[1 + i], dp, ctx).wait_recv()
        stats = merged(tbuf[...].reshape(8, 384))
        in_heads = lanes < T_HEADS
        above, below = stats[:, 256:], jnp.where(in_heads, stats[:, 128:256], 1.0)
        t_score = jnp.sum(jnp.where(in_heads, above / below, 0.0), axis=1, keepdims=True)
        trow[...] = jnp.where(k == 0, jnp.broadcast_to(t_score, (1, 128)), 0.0)
        for i in range(6):
            remote(cstage, cbuf.at[i], c_send, c_recv.at[i], dp, ctx).wait_recv()
        cstage[...] = cstage[...] + jnp.sum(cbuf[...].reshape(6, D), axis=0, keepdims=True)

    def p_copy(d):
        return remote(pbuf.at[root], pbuf.at[root], p_send.at[d], p_recv.at[root], dp, line + (pos + d) % 16)

    spot = 4 * x + y

    def r_copy(d):
        there = (spot + d) % 16
        return remote(
            rbuf.at[spot], rbuf.at[spot], r_send.at[d], r_recv.at[d], 2 * (there // 4) + zh, 16 * (there % 4) + pos
        )

    deep = 16 * zh + pos

    def s_copy(d):
        there = (deep + d) % 32
        slot = sbuf.at[4 * zh + root]
        return remote(slot, slot, s_send.at[d], s_recv.at[4 * zh + root], 2 * x + there // 16, line + there % 16)

    @pl.when(c >= 6)
    def _():
        mean = cstage[...] / length.astype(F32)
        student = jnp.sum(mean * shead_ref[...], axis=1, keepdims=True)
        rbuf[spot] = jnp.where(lanes == thread, student, 0.0) + jnp.where(lanes == 64 + thread, trow[...], 0.0)
        for d in range(1, 16):
            r_copy(d).start()
        pbuf[root] = jnp.concatenate([mean, trow[...]], axis=1)
        for d in range(1, 16):
            p_copy(d).start()
        for d in range(1, 16):
            ref = rbuf.at[(spot + 16 - d) % 16]
            remote(ref, ref, r_send.at[0], r_recv.at[d], dp, ctx).wait_recv()
        sbuf[4 * zh + root] = jnp.sum(rbuf[...].reshape(16, 128), axis=0, keepdims=True)
        for d in range(1, 32):
            s_copy(d).start()

    for r in range(4):

        @pl.when(pos != 12 + r)
        def _():
            ref = pbuf.at[r]
            remote(ref, ref, p_send.at[0], p_recv.at[r], dp, ctx).wait_recv()

    ybuf[y] = (pbuf[0] + pbuf[1]) + (pbuf[2] + pbuf[3])

    def y_copy(d):
        return remote(ybuf.at[y], ybuf.at[y], y_send.at[d], y_recv.at[d], dp, y_peer(d))

    for d in range(1, 4):
        y_copy(d).start()

    def sent(b, carry):
        for q in range(4):

            @pl.when(jnp.logical_or(passes_on(b), passes_back(b)))
            def _():
                ring_copy(b, q).wait_send()

            sib_copy(b, q).wait_send()
        return carry

    lax.fori_loop(0, c + 1, sent, 0)

    @pl.when(c <= 1)
    def _():
        for q in range(4):
            rev_copy(q).wait_send()

    @pl.when(c == 4)
    def _():
        for r in range(2):
            for q in range(4):
                relay_copy(r, q).wait_send()

    for gather in (gk, gv, gq, go):
        gather.finish()
    t_copy().wait_send()

    @pl.when(c != 6)
    def _():
        t_gather().wait_send()

    @pl.when(c <= 5)
    def _():
        chain_copy().wait_send()

    @pl.when(c >= 6)
    def _():
        for d in range(1, 16):
            r_copy(d).wait_send()
            p_copy(d).wait_send()

    for d in range(1, 4):
        ref = ybuf.at[(y + 4 - d) % 4]
        remote(ref, ref, y_send.at[0], y_recv.at[d], dp, ctx).wait_recv()
    rows = jnp.concatenate([ybuf[i] for i in range(4)], axis=0)
    pooled_ref[...] = rows[:, :D]
    eye4 = lax.broadcasted_iota(jnp.int32, (4, 4), 0) == lax.broadcasted_iota(jnp.int32, (4, 4), 1)
    tscore_ref[...] = jnp.sum(jnp.where(eye4, rows[:, D : D + 4], 0.0), axis=0, keepdims=True)
    for d in range(1, 4):
        y_copy(d).wait_send()

    for r in range(8):

        @pl.when(deep != 12 + r + 12 * (r // 4))
        def _():
            ref = sbuf.at[r]
            remote(ref, ref, s_send.at[0], s_recv.at[r], dp, ctx).wait_recv()

    every = jnp.sum(sbuf[...].reshape(8, 128), axis=0, keepdims=True)
    threads = list_ref.shape[1]
    student_all, teacher_all = every[:, :threads], every[:, 64 : 64 + threads]
    target = teacher_all + rel_ref[...].astype(F32)
    member = lax.broadcasted_iota(jnp.int32, (8, threads), 0) == list_ref[...]

    def log_soft(logits):
        masked = jnp.where(member, logits, BIG)
        top = jnp.max(masked, axis=1, keepdims=True)
        shifted = jnp.where(member, jnp.exp(masked - top), 0.0)
        return masked - top - jnp.log(jnp.sum(shifted, axis=1, keepdims=True))

    target_log = log_soft(target)
    student_log = log_soft(student_all)
    target_prob = jnp.where(member, jnp.exp(target_log), 0.0)
    terms = jnp.where(member, target_prob * (target_log - student_log), 0.0)
    div_column = jnp.sum(terms, axis=1, keepdims=True)
    eye8 = lax.broadcasted_iota(jnp.int32, (8, 8), 0) == lax.broadcasted_iota(jnp.int32, (8, 8), 1)
    div_ref[...] = jnp.sum(jnp.where(eye8, div_column, 0.0), axis=0, keepdims=True)

    @pl.when(c >= 6)
    def _():
        for d in range(1, 32):
            s_copy(d).wait_send()


def place(out, pooled, tscore, div, out_ref, pooled_ref, tscore_ref, div_ref):
    out_ref[...] = out[...]
    pooled_ref[...] = pooled[...]
    tscore_ref[...] = tscore[...]
    div_ref[...] = div[...]


def local(
    student_hidden, w_query, w_keyval, w_out, norm_gain, student_head, teacher_query, teacher_keys, teacher_values,
    teacher_head, thread_lengths, list_index, relevance,
):
    vmem = pl.BlockSpec(memory_space=pltpu.VMEM)
    anywhere = pl.BlockSpec(memory_space=pl.ANY)
    dma = pltpu.SemaphoreType.DMA
    out, pooled, tscore, div = pl.pallas_call(
        kernel,
        out_shape=(
            jax.ShapeDtypeStruct((ROWS, D), F32),
            jax.ShapeDtypeStruct((4, D), F32),
            jax.ShapeDtypeStruct((1, 4), F32),
            jax.ShapeDtypeStruct((1, 8), F32),
        ),
        in_specs=[anywhere] * 13,
        out_specs=(vmem,) * 4,
        scratch_shapes=[
            pltpu.VMEM((ROWS, D), BF16),
            pltpu.VMEM((4, 2, 128, 256), BF16),
            pltpu.VMEM((4, 2, 128, 256), BF16),
            pltpu.VMEM((4, 2, 128, D), BF16),
            pltpu.VMEM((4, 2, 128, D), BF16),
            pltpu.VMEM((ROWS, 2048), BF16),
            pltpu.VMEM((ROWS, 2048), BF16),
            pltpu.VMEM((16, 4, 256, 128), BF16),
            pltpu.VMEM((2, 4, 256, 128), BF16),
            pltpu.VMEM((KV_HEADS, GROUPS, HD, ROWS), BF16),
            pltpu.VMEM((ROWS, D), BF16),
            pltpu.VMEM((HEADS, 1, ROWS), F32),
            pltpu.VMEM((HEADS, 1, ROWS), F32),
            pltpu.VMEM((HEADS, HD, ROWS), F32),
            pltpu.VMEM((2, 1, 384), F32),
            pltpu.VMEM((8, 1, 384), F32),
            pltpu.VMEM((1, 128), F32),
            pltpu.VMEM((6, 1, D), F32),
            pltpu.VMEM((1, D), F32),
            pltpu.VMEM((4, 1, D + 128), F32),
            pltpu.VMEM((16, 1, 128), F32),
            pltpu.VMEM((4, 1, D + 128), F32),
            pltpu.VMEM((8, 1, 128), F32),
            pltpu.VMEM((2, ROWS, 256), F32),
            pltpu.VMEM((1, D), F32),
            pltpu.VMEM((1, D), F32),
            pltpu.VMEM((4, 2048), BF16),
            pltpu.VMEM((1, 2048), F32),
            pltpu.SMEM((32,), jnp.int32),
            pltpu.VMEM((1, 32), jnp.int32),
            pltpu.VMEM((1, 32), jnp.int32),
            dma((14,)),
            dma((4, 17)),
            dma((4, 14)),
            dma((16, 4)),
            dma((8, 4)),
            dma((8, 4)),
            dma((4,)),
            dma((2, 4)),
            dma((2, 4)),
            dma((2,)),
            dma((9,)),
            dma,
            dma((6,)),
            dma((16,)),
            dma((4,)),
            dma((16,)),
            dma((16,)),
            dma((4,)),
            dma((4,)),
            dma((32,)),
            dma((8,)),
        ],
        compiler_params=pltpu.CompilerParams(
            collective_id=0, has_side_effects=True, vmem_limit_bytes=60 * 1024 * 1024
        ),
        cost_estimate=pl.CostEstimate(flops=10**10, bytes_accessed=8 * 2**20, transcendentals=8 * 10**6),
    )(
        student_hidden, w_keyval, w_query, w_out, norm_gain.reshape(1, -1), student_head.reshape(1, -1), teacher_query,
        teacher_keys, teacher_values, teacher_head.reshape(1, -1), thread_lengths, list_index.reshape(1, -1),
        relevance.reshape(1, -1),
    )
    out, pooled, tscore, div = pl.pallas_call(
        place,
        out_shape=tuple(jax.ShapeDtypeStruct(a.shape, a.dtype) for a in (out, pooled, tscore, div)),
        in_specs=[vmem] * 4,
        out_specs=(vmem,) * 4,
        compiler_params=pltpu.CompilerParams(vmem_limit_bytes=60 * 1024 * 1024),
    )(out, pooled, tscore, div)
    return out, pooled, tscore.reshape(4), div.reshape(8)


def solution(mesh):
    return jax.shard_map(
        local,
        mesh=mesh,
        in_specs=(
            P(("dp", "ctx"), None), P("dp", None), P("dp", None), P("dp", None), P(), P(), P("dp", None),
            P(("dp", "ctx"), None), P(("dp", "ctx"), None), P(), P(), P(), P(),
        ),
        out_specs=(P(("dp", "ctx"), None), P("dp", None), P("dp"), P()),
        check_vma=False,
    )
```

```python
import functools

import jax
import jax.numpy as jnp
from jax import lax
from jax.experimental import pallas as pl
from jax.experimental.pallas import tpu as pltpu
from jax.sharding import PartitionSpec as P

HEADS = 8
KV_HEADS = 2
GROUPS = 4
HD = 128
T_HEADS = 16
ROWS = 256
D = 1024
CHIPS = 8
BIG = -1e30
F32 = jnp.float32
BF16 = jnp.bfloat16
SCALE = HD ** (-0.5)
LOG2E = 1.4426950408889634
MESH = pl.DeviceIdType.MESH


def kernel(
    hid_in, wkv_in, wq_in, wo_in, gain_in, shead_in, tq_in, tk_in, tv_in, thead_in, len_in, list_in, rel_in,
    out_ref, pooled_ref, tscore_ref, div_ref,
    hid, wk, wv, wq, wo, tk, tv, kvb, relay, qt, att, m_ref, l_ref, acc_ref,
    tsib, tbuf, trow, cbuf, cstage, pbuf, rbuf, ybuf, sbuf, kv_part,
    gain_ref, shead_ref, tq_ref, thead_ref, len_ref, list_ref, rel_ref,
    lsem, wsend, wrecv, kv_recv, kv_send, sib_send, rev_send, relay_recv, relay_send,
    t_send, t_recv, c_send, c_recv, p_send, p_recv, r_send, r_recv, y_send, y_recv, s_send, s_recv,
):
    dp = lax.axis_index("dp")
    ctx = lax.axis_index("ctx")
    x, zh = dp // 2, dp % 2
    y, pos = ctx // 16, ctx % 16
    c, k = pos // 2, pos % 2
    oz = 1 - zh
    other_dp = 2 * x + oz
    sib_ctx = ctx + 1 - 2 * k
    line = y * 16

    def remote(src, dst, ssem, rsem, to_dp, to_ctx):
        return pltpu.make_async_remote_copy(
            src_ref=src, dst_ref=dst, send_sem=ssem, recv_sem=rsem, device_id=(to_dp, to_ctx), device_id_type=MESH
        )

    def x_peer(d):
        return 2 * ((x + d) % 4) + zh

    def y_peer(d):
        return ((y + d) % 4) * 16 + pos

    thread = dp * 4 + y

    lane = 64 * k
    locals_ = [
        pltpu.make_async_copy(hid_in, hid, lsem.at[0]),
        pltpu.make_async_copy(tk_in, tk, lsem.at[1]),
        pltpu.make_async_copy(tv_in, tv, lsem.at[2]),
    ]
    weights = [(wkv_in.at[:, pl.ds(0, 256)], wk), (wkv_in.at[:, pl.ds(256, 256)], wv), (wq_in, wq), (wo_in, wo)]
    for i, (w_in, w) in enumerate(weights):
        locals_.append(
            pltpu.make_async_copy(w_in.at[pl.ds(lane, 64)], w.at[x, zh, pl.ds(lane, 64)], lsem.at[3 + i])
        )
    small = [
        (gain_in, gain_ref), (shead_in, shead_ref), (tq_in, tq_ref), (thead_in, thead_ref), (len_in, len_ref),
        (list_in, list_ref), (rel_in, rel_ref),
    ]
    small = [pltpu.make_async_copy(src, dst, lsem.at[7 + i]) for i, (src, dst) in enumerate(small)]
    for copy in [locals_[0]] + locals_[3:] + locals_[1:3]:
        copy.start()
    for copy in small:
        copy.start()

    barrier = pltpu.get_barrier_semaphore()

    def greet(to_dp, to_ctx):
        pl.semaphore_signal(barrier, inc=1, device_id=(to_dp, to_ctx), device_id_type=MESH)

    greet(dp, sib_ctx)
    for d in range(1, 4):
        greet(dp, y_peer(d))
        greet(x_peer(d), ctx)

    @pl.when(c < 7)
    def _():
        greet(dp, ctx + 2)

    @pl.when(c > 0)
    def _():
        greet(dp, ctx - 2)

    @pl.when(c == 0)
    def _():
        for j in range(4, 8):
            greet(other_dp, line + 2 * j + k)

    @pl.when(c == 7)
    def _():
        for j in range(5):
            greet(other_dp, line + 2 * j + k)

    @pl.when(jnp.logical_and(c >= 1, c <= 4))
    def _():
        greet(other_dp, line + 14 + k)

    @pl.when(jnp.logical_and(c >= 4, c <= 6))
    def _():
        greet(other_dp, line + k)

    @pl.when(c == 1)
    def _():
        greet(other_dp, line + 8 + k)

    @pl.when(c == 4)
    def _():
        greet(other_dp, line + 2 + k)

    def least(value, n):
        return (value + 8 - n) // 8

    @pl.when(c == 6)
    def _():
        for j in range(5):
            greet(dp, line + 2 * j + k)

    more = 3 - 2 * least(c, 1) - least(c, 2) + 2 * least(c, 4) - 2 * least(c, 5) + 4 * least(c, 7)
    pl.semaphore_wait(barrier, 10 + least(c, 1) - least(c, 5) - least(c, 7) + more)

    class Gather:
        def __init__(self, i):
            self.i = i
            self.w_in, self.w = weights[i]
            self.piece = 64 * k + 16 * y
            self.ring, self.fine = i >= 2, i == 0

        def sem(self, table, n):
            return table.at[self.i, n]

        def z_copy(self, j):
            w = self.w.at[x, zh, pl.ds(self.piece, 16)]
            return remote(
                self.w_in.at[pl.ds(self.piece, 16)], w, self.sem(wsend, j % 4), self.sem(wrecv, 0),
                other_dp, line + 2 * j + k,
            )

        def z_start(self):
            @pl.when(c == 0)
            def _():
                for j in range(4, 8):
                    self.z_copy(j).start()

            @pl.when(c == 7)
            def _():
                for j in range(4):
                    self.z_copy(j).start()

        def z_recv(self):
            w = self.w.at[x, oz, pl.ds(self.piece, 16)]
            remote(w, w, self.sem(wsend, 0), self.sem(wrecv, 0), other_dp, ctx).wait_recv()

        def own_part(self, at, first=0, rows=64):
            return self.w.at[(x + at) % 4, zh, pl.ds(lane + first, rows)]

        def own_copies(self):
            src = self.w_in.at[pl.ds(lane, 64)]
            hops = (1, 3) if self.ring else (1, 2, 3)
            return [
                remote(src, self.own_part(0), self.sem(wsend, 3 + d), self.sem(wrecv, d), x_peer(d), ctx) for d in hops
            ]

        def own_relays(self):
            left, right = self.own_part(3, 0, 32), self.own_part(1, 32, 32)
            return [
                remote(left, left, self.sem(wsend, 5), self.sem(wrecv, 2), x_peer(1), ctx),
                remote(right, right, self.sem(wsend, 15), self.sem(wrecv, 12), x_peer(3), ctx),
            ]

        def own_start(self):
            for copy in self.own_copies():
                copy.start()

        def arrived(self, w, n):
            remote(w, w, self.sem(wsend, 0), self.sem(wrecv, n), dp, ctx).wait_recv()

        def own_mid(self):
            relays = self.own_relays()
            self.arrived(self.own_part(3), 1)
            relays[0].start()
            self.arrived(self.own_part(1), 3)
            relays[1].start()

        def own_recv(self):
            if self.ring:
                self.arrived(self.own_part(2, 0, 32), 2)
                self.arrived(self.own_part(2, 32, 32), 12)
            else:
                for d in range(1, 4):
                    self.arrived(self.own_part(4 - d), d)

        def other_copy(self, d):
            w = self.w.at[x, oz, pl.ds(self.piece, 16)]
            return remote(w, w, self.sem(wsend, 6 + d), self.sem(wrecv, 3 + d), x_peer(d), ctx)

        def other_start(self):
            for d in range(1, 4):
                self.other_copy(d).start()

        def other_recv(self):
            for d in range(1, 4):
                self.arrived(self.w.at[(x + 4 - d) % 4, oz, pl.ds(self.piece, 16)], 3 + d)

        def y_part(self, at, first=0, count=4):
            return self.w.at[pl.ds(first, count), oz, pl.ds(64 * k + 16 * ((y + at) % 4), 16)]

        def y_copies(self):
            src = self.y_part(0)
            hops = (1, 3) if self.ring else (1, 2, 3)
            return [remote(src, src, self.sem(wsend, 9 + d), self.sem(wrecv, 6 + d), dp, y_peer(d)) for d in hops]

        def y_relays(self):
            left, right = self.y_part(3, 0, 2), self.y_part(1, 2, 2)
            return [
                remote(left, left, self.sem(wsend, 11), self.sem(wrecv, 8), dp, y_peer(1)),
                remote(right, right, self.sem(wsend, 16), self.sem(wrecv, 13), dp, y_peer(3)),
            ]

        def fine_copy(self, at, d):
            w = self.w.at[(x + at) % 4, oz, pl.ds(self.piece, 16)]
            n = 3 * at + d
            return remote(w, w, self.sem(wsend, 16 + n), self.sem(wrecv, 13 + n), dp, y_peer(d))

        def fine_start(self, at):
            for d in range(1, 4):
                self.fine_copy(at, d).start()

        def fine_rest(self):
            for d in (1, 3, 2):
                self.arrived(self.w.at[(x + 4 - d) % 4, oz, pl.ds(self.piece, 16)], 3 + d)
                self.fine_start(4 - d)

        def fine_recv(self):
            for at in range(4):
                for d in range(1, 4):
                    w = self.w.at[(x + at) % 4, oz, pl.ds(64 * k + 16 * ((y + 4 - d) % 4), 16)]
                    self.arrived(w, 13 + 3 * at + d)

        def y_start(self):
            for copy in self.y_copies():
                copy.start()

        def y_mid(self):
            relays = self.y_relays()
            self.arrived(self.y_part(3), 7)
            relays[0].start()
            self.arrived(self.y_part(1), 9)
            relays[1].start()

        def y_recv(self):
            if self.ring:
                self.arrived(self.y_part(2, 0, 2), 8)
                self.arrived(self.y_part(2, 2, 2), 13)
            else:
                for d in range(1, 4):
                    self.arrived(self.y_part(4 - d), 6 + d)

        def sib_copy(self, half, n):
            w = self.w.at[:, half, pl.ds(lane, 64)]
            return remote(w, w, self.sem(wsend, 13 + n), self.sem(wrecv, 10 + n), dp, sib_ctx)

        def sib_recv(self, half, n):
            w = self.w.at[:, half, pl.ds(64 - lane, 64)]
            remote(w, w, self.sem(wsend, 0), self.sem(wrecv, 10 + n), dp, ctx).wait_recv()

        def finish(self):
            @pl.when(c == 0)
            def _():
                for j in range(4, 8):
                    self.z_copy(j).wait_send()

            @pl.when(c == 7)
            def _():
                for j in range(4):
                    self.z_copy(j).wait_send()

            copies = self.own_copies() + [self.other_copy(d) for d in range(1, 4)]
            if self.fine:
                copies += [self.fine_copy(at, d) for at in range(4) for d in range(1, 4)]
            else:
                copies += self.y_copies()
            for copy in copies + (self.own_relays() + self.y_relays() if self.ring else []):
                copy.wait_send()
            self.sib_copy(zh, 0).wait_send()
            self.sib_copy(oz, 1).wait_send()

    for copy in small:
        copy.wait()
    length = len_ref[thread]
    gk, gv, gq, go = (Gather(i) for i in range(4))

    gk.z_start()
    gk.own_start()
    gv.z_start()
    gk.z_recv()
    gk.other_start()
    gk.fine_start(0)
    gv.own_start()
    gv.z_recv()
    gv.other_start()
    gq.z_start()
    go.z_start()
    gk.own_recv()
    locals_[3].wait()
    gk.sib_copy(zh, 0).start()
    gk.fine_rest()
    gv.other_recv()
    gv.y_start()
    gv.own_recv()
    locals_[4].wait()
    gv.sib_copy(zh, 0).start()
    gq.own_start()
    locals_[0].wait()

    def project(half, w):
        parts = [hid[:, pl.ds(pl.multiple_of((2 * i + half) * 128, 128), 128)] for i in range(4)]
        return jnp.dot(jnp.concatenate(parts, axis=1), w[:, half].reshape(512, 256), preferred_element_type=F32)

    gk.sib_recv(zh, 0)
    kv_part[0] = project(zh, wk)
    gq.z_recv()
    gq.other_start()
    gk.fine_recv()
    gk.sib_copy(oz, 1).start()
    gv.sib_recv(zh, 0)
    kv_part[1] = project(zh, wv)
    own = 2 * c + k

    def hand(b, q, ssem, to_ctx):
        ref = kvb.at[2 * b + k, q]
        return remote(ref, ref, ssem.at[b, q], kv_recv.at[2 * b + k, q], dp, to_ctx)

    def ring_copy(b, q):
        return hand(b, q, kv_send, ctx + 2)

    def back_copy(b, q):
        return hand(b, q, kv_send, ctx - 2)

    def sib_copy(b, q):
        return hand(b, q, sib_send, sib_ctx)

    def kv_wait(block, q):
        ref = kvb.at[block, q]
        remote(ref, ref, kv_send.at[0, 0], kv_recv.at[block, q], dp, ctx).wait_recv()

    def rev_copy(q):
        return remote(
            kvb.at[own, q], relay.at[c, q], rev_send.at[q], relay_recv.at[c, q], other_dp, line + 8 + k
        )

    def relay_copy(r, q):
        return remote(
            relay.at[r, q], kvb.at[2 * r + k, q], relay_send.at[r, q], kv_recv.at[2 * r + k, q], other_dp, line + 14 + k
        )

    def passes_on(b):
        gap = jnp.logical_or(jnp.logical_and(b == 0, c >= 4), jnp.logical_and(b == 1, c >= 6))
        return jnp.logical_and(c < 7, jnp.logical_not(gap))

    def passes_back(b):
        return jnp.logical_and(b == 0, c >= 6)

    def send_own(q):
        @pl.when(c < 7)
        def _():
            ring_copy(c, q).start()

        @pl.when(c == 0)
        def _():
            rev_copy(q).start()

        sib_copy(c, q).start()

    gk.sib_recv(oz, 1)
    keys = (kv_part[0] + project(oz, wk)).astype(BF16)
    for h in range(KV_HEADS):
        kvb[own, h] = keys[:, h * HD : (h + 1) * HD]
        send_own(h)
    gv.y_recv()
    gv.sib_copy(oz, 1).start()
    gv.sib_recv(oz, 1)
    values = (kv_part[1] + project(oz, wv)).astype(BF16)
    for h in range(KV_HEADS):
        for part in range(2):
            kvb[own, 2 + h, pl.ds(part * 128, 128)] = values[part * 128 : (part + 1) * 128, h * HD : (h + 1) * HD].T
        send_own(2 + h)

    def block_at(s):
        last = -4 * least(s, 3) + 5 * least(s, 4) - least(s, 6) + 2 * least(s, 7)
        before = -2 * least(s, 4) + 3 * least(s, 5)
        return c - s + last * least(c, 7) + before * (least(c, 6) - least(c, 7))

    def forward(s, j):
        b = block_at(s)

        @pl.when(s <= c)
        def _():
            for q in (2 * j, 2 * j + 1):
                kv_wait(2 * b + k, q)

                @pl.when(passes_on(b))
                def _():
                    ring_copy(b, q).start()

                @pl.when(passes_back(b))
                def _():
                    back_copy(b, q).start()

                sib_copy(b, q).start()

    def relay_on(r, j):
        @pl.when(c == 4)
        def _():
            for q in (2 * j, 2 * j + 1):
                ref = relay.at[r, q]
                remote(ref, ref, rev_send.at[q], relay_recv.at[r, q], dp, ctx).wait_recv()
                relay_copy(r, q).start()

    def attend(b, h, diag):
        kp = jnp.concatenate([kvb[2 * b, h], kvb[2 * b + 1, h]], axis=0)
        v0, v1 = kvb[2 * b, 2 + h], kvb[2 * b + 1, 2 + h]
        vt = jnp.concatenate([v0[:128], v0[128:], v1[:128], v1[128:]], axis=1)
        queries = jnp.concatenate([qt[h, g] for g in range(GROUPS)], axis=1)
        wide = jnp.dot(kp, queries, preferred_element_type=F32) * (SCALE * LOG2E)
        for g in range(GROUPS):
            i = h * GROUPS + g
            s = wide[:, g * ROWS : (g + 1) * ROWS]
            if diag:
                key = lax.broadcasted_iota(jnp.int32, (2 * ROWS, ROWS), 0)
                row = lax.broadcasted_iota(jnp.int32, (2 * ROWS, ROWS), 1)
                s = jnp.where(key <= k * ROWS + row, s, BIG)
            best = jnp.max(s, axis=0, keepdims=True)
            if not diag:
                old = m_ref[i]
                best = jnp.maximum(old, best)
                carry = jnp.exp2(old - best)
            p = jnp.exp2(s - best)
            total = jnp.sum(p, axis=0, keepdims=True)
            out = jnp.dot(vt, p.astype(BF16), preferred_element_type=F32)
            m_ref[i] = best
            if diag:
                l_ref[i] = total
                acc_ref[i] = out
            else:
                l_ref[i] = l_ref[i] * carry + total
                acc_ref[i] = acc_ref[i] * carry + out

    gq.own_mid()
    gq.other_recv()
    gq.y_start()
    slot_row = lax.broadcasted_iota(jnp.int32, (4, 2048), 0) == y
    own_q = jnp.sum(jnp.where(slot_row, tq_ref[...].astype(F32), 0.0), axis=0, keepdims=True)
    head_of = lax.broadcasted_iota(jnp.int32, (T_HEADS, 2048), 1) // HD
    diagonal = head_of == lax.broadcasted_iota(jnp.int32, (T_HEADS, 2048), 0)
    q_heads = jnp.where(diagonal, own_q, 0.0).astype(BF16)
    locals_[1].wait()
    ts = lax.dot_general(q_heads, tk[...], (((1,), (1,)), ((), ())), preferred_element_type=F32) * SCALE
    t_valid = pos * ROWS + lax.broadcasted_iota(jnp.int32, (T_HEADS, ROWS), 1) < length
    ts = jnp.where(t_valid, ts, BIG)
    t_best = jnp.max(ts, axis=1, keepdims=True)
    t_weights = jnp.where(t_valid, jnp.exp(ts - t_best), 0.0)
    t_total = jnp.sum(t_weights, axis=1, keepdims=True)
    locals_[2].wait()
    t_out = jnp.dot(t_weights.astype(BF16), tv[...], preferred_element_type=F32)
    t_sum = jnp.sum(jnp.where(diagonal, t_out * thead_ref[...], 0.0), axis=1, keepdims=True)
    eye = lax.broadcasted_iota(jnp.int32, (T_HEADS, 128), 0) == lax.broadcasted_iota(jnp.int32, (T_HEADS, 128), 1)

    def row_of(column):
        return jnp.sum(jnp.where(eye, column, 0.0), axis=0, keepdims=True)

    tsib[k] = jnp.concatenate([row_of(t_best), row_of(t_total), row_of(t_sum)], axis=1)

    def t_copy():
        return remote(tsib.at[k], tsib.at[k], t_send.at[0], t_recv.at[0], dp, sib_ctx)

    def merged(rows):
        best = jnp.max(rows[:, :128], axis=0, keepdims=True)
        factor = jnp.exp(rows[:, :128] - best)
        sums = [jnp.sum(rows[:, n : n + 128] * factor, axis=0, keepdims=True) for n in (128, 256)]
        return jnp.concatenate([best] + sums, axis=1)

    def t_gather():
        return remote(tbuf.at[c], tbuf.at[c], t_send.at[1], t_recv.at[1 + c], dp, line + 12 + k)

    t_copy().start()

    gq.own_recv()
    locals_[5].wait()
    gq.sib_copy(zh, 0).start()
    go.own_start()
    forward(1, 0)
    relay_on(0, 0)
    gq.y_mid()
    forward(1, 1)
    relay_on(0, 1)

    @pl.when(c == 1)
    def _():
        for q in range(4):
            rev_copy(q).start()

    go.z_recv()
    go.other_start()
    gq.y_recv()
    gq.sib_copy(oz, 1).start()
    forward(2, 0)
    gq.sib_recv(zh, 0)
    gq.sib_recv(oz, 1)
    query = jnp.dot(hid[...], wq[...].reshape(D, HEADS * HD), preferred_element_type=F32).astype(BF16)
    for i in range(HEADS):
        qt[i // GROUPS, i % GROUPS] = query[:, i * HD : (i + 1) * HD].T
    forward(2, 1)
    remote(tsib.at[1 - k], tsib.at[1 - k], t_send.at[0], t_recv.at[0], dp, ctx).wait_recv()
    tbuf[c] = merged(jnp.concatenate([tsib[0], tsib[1]], axis=0))

    @pl.when(c != 6)
    def _():
        t_gather().start()

    go.own_mid()
    for h in range(KV_HEADS):
        for q in (h, 2 + h):
            kv_wait(2 * c + 1 - k, q)
        attend(c, h, True)
    go.other_recv()
    go.y_start()

    def first_part(u):
        return u - 1 - (9 - u) * (1 - (u + 7) // 16)

    def part(a, carry):
        pair, h = a // 2, a % 2

        @pl.when(pair <= c)
        def _():
            b = block_at(pair)
            for j in range(2):
                kv_wait(2 * b + 1 - k, 2 * j + h)
            attend(b, h, False)

        return carry

    def step(s, carry):
        for j in range(2):
            forward(s, j)

            @pl.when(s == 3)
            def _():
                relay_on(1, j)

            u = 2 * s + j
            lax.fori_loop(first_part(u), first_part(u + 1), part, 0)

        @pl.when(s == 3)
        def _():
            go.own_recv()
            locals_[6].wait()
            go.sib_copy(zh, 0).start()

        @pl.when(s == 4)
        def _():
            go.y_mid()

        @pl.when(s == 5)
        def _():
            go.y_recv()
            go.sib_copy(oz, 1).start()

        return carry

    lax.fori_loop(3, 8, step, 0)
    part(15, 0)

    for i in range(HEADS):
        att[:, i * HD : (i + 1) * HD] = (acc_ref[i] / l_ref[i]).astype(BF16).T
    go.sib_recv(zh, 0)
    go.sib_recv(oz, 1)
    hidden = hid[...].astype(F32) + jnp.dot(att[...], wo[...].reshape(D, D), preferred_element_type=F32)
    valid = pos * ROWS + lax.broadcasted_iota(jnp.int32, (ROWS, 1), 0) < length
    rate = jnp.where(valid, lax.rsqrt(jnp.mean(hidden * hidden, axis=1, keepdims=True) + 1e-05), 0.0)
    part = jnp.sum(hidden * rate, axis=0, keepdims=True) * gain_ref[...]
    out_ref[...] = jnp.where(valid, hidden, 0.0)

    def chain_copy():
        return remote(cstage, cbuf.at[c], c_send, c_recv.at[c], dp, line + 12 + k)

    cstage[...] = part

    @pl.when(c <= 5)
    def _():
        chain_copy().start()

    root = 2 * (c - 6) + k
    lanes = lax.broadcasted_iota(jnp.int32, (1, 128), 1)

    @pl.when(c == 7)
    def _():
        trow[...] = jnp.zeros_like(trow)

    @pl.when(c == 6)
    def _():
        for i in (0, 1, 2, 3, 4, 5, 7):
            remote(tbuf.at[i], tbuf.at[i], t_send.at[0], t_recv.at[1 + i], dp, ctx).wait_recv()
        stats = merged(tbuf[...].reshape(8, 384))
        in_heads = lanes < T_HEADS
        above, below = stats[:, 256:], jnp.where(in_heads, stats[:, 128:256], 1.0)
        t_score = jnp.sum(jnp.where(in_heads, above / below, 0.0), axis=1, keepdims=True)
        trow[...] = jnp.where(k == 0, jnp.broadcast_to(t_score, (1, 128)), 0.0)
        for i in range(6):
            remote(cstage, cbuf.at[i], c_send, c_recv.at[i], dp, ctx).wait_recv()
        cstage[...] = cstage[...] + jnp.sum(cbuf[...].reshape(6, D), axis=0, keepdims=True)

    def p_copy(d):
        return remote(pbuf.at[root], pbuf.at[root], p_send.at[d], p_recv.at[root], dp, line + (pos + d) % 16)

    spot = 4 * x + y

    def r_copy(d):
        there = (spot + d) % 16
        return remote(
            rbuf.at[spot], rbuf.at[spot], r_send.at[d], r_recv.at[d], 2 * (there // 4) + zh, 16 * (there % 4) + pos
        )

    deep = 16 * zh + pos

    def s_copy(d):
        there = (deep + d) % 32
        slot = sbuf.at[4 * zh + root]
        return remote(slot, slot, s_send.at[d], s_recv.at[4 * zh + root], 2 * x + there // 16, line + there % 16)

    @pl.when(c >= 6)
    def _():
        mean = cstage[...] / length.astype(F32)
        student = jnp.sum(mean * shead_ref[...], axis=1, keepdims=True)
        rbuf[spot] = jnp.where(lanes == thread, student, 0.0) + jnp.where(lanes == 64 + thread, trow[...], 0.0)
        for d in sorted(range(1, 16), key=lambda d: -min(d // 4, 4 - d // 4) - min(d % 4, 4 - d % 4)):
            r_copy(d).start()
        pbuf[root] = jnp.concatenate([mean, trow[...]], axis=1)
        for d in range(1, 16):
            p_copy(d).start()
        for d in range(1, 16):
            ref = rbuf.at[(spot + 16 - d) % 16]
            remote(ref, ref, r_send.at[0], r_recv.at[d], dp, ctx).wait_recv()
        sbuf[4 * zh + root] = jnp.sum(rbuf[...].reshape(16, 128), axis=0, keepdims=True)
        for d in sorted(range(1, 32), key=lambda d: abs(d - 16)):
            s_copy(d).start()

    for r in range(4):

        @pl.when(pos != 12 + r)
        def _():
            ref = pbuf.at[r]
            remote(ref, ref, p_send.at[0], p_recv.at[r], dp, ctx).wait_recv()

    ybuf[y] = (pbuf[0] + pbuf[1]) + (pbuf[2] + pbuf[3])

    def y_copy(d):
        return remote(ybuf.at[y], ybuf.at[y], y_send.at[d], y_recv.at[d], dp, y_peer(d))

    for d in range(1, 4):
        y_copy(d).start()

    def sent(b, carry):
        for q in range(4):

            @pl.when(jnp.logical_or(passes_on(b), passes_back(b)))
            def _():
                ring_copy(b, q).wait_send()

            sib_copy(b, q).wait_send()
        return carry

    lax.fori_loop(0, c + 1, sent, 0)

    @pl.when(c <= 1)
    def _():
        for q in range(4):
            rev_copy(q).wait_send()

    @pl.when(c == 4)
    def _():
        for r in range(2):
            for q in range(4):
                relay_copy(r, q).wait_send()

    for gather in (gk, gv, gq, go):
        gather.finish()
    t_copy().wait_send()

    @pl.when(c != 6)
    def _():
        t_gather().wait_send()

    @pl.when(c <= 5)
    def _():
        chain_copy().wait_send()

    @pl.when(c >= 6)
    def _():
        for d in range(1, 16):
            r_copy(d).wait_send()
            p_copy(d).wait_send()

    for d in range(1, 4):
        ref = ybuf.at[(y + 4 - d) % 4]
        remote(ref, ref, y_send.at[0], y_recv.at[d], dp, ctx).wait_recv()
    rows = jnp.concatenate([ybuf[i] for i in range(4)], axis=0)
    pooled_ref[...] = rows[:, :D]
    eye4 = lax.broadcasted_iota(jnp.int32, (4, 4), 0) == lax.broadcasted_iota(jnp.int32, (4, 4), 1)
    tscore_ref[...] = jnp.sum(jnp.where(eye4, rows[:, D : D + 4], 0.0), axis=0, keepdims=True)
    for d in range(1, 4):
        y_copy(d).wait_send()

    for r in range(8):

        @pl.when(deep != 12 + r + 12 * (r // 4))
        def _():
            ref = sbuf.at[r]
            remote(ref, ref, s_send.at[0], s_recv.at[r], dp, ctx).wait_recv()

    every = jnp.sum(sbuf[...].reshape(8, 128), axis=0, keepdims=True)
    threads = list_ref.shape[1]
    student_all, teacher_all = every[:, :threads], every[:, 64 : 64 + threads]
    target = teacher_all + rel_ref[...].astype(F32)
    member = lax.broadcasted_iota(jnp.int32, (8, threads), 0) == list_ref[...]

    def log_soft(logits):
        masked = jnp.where(member, logits, BIG)
        top = jnp.max(masked, axis=1, keepdims=True)
        shifted = jnp.where(member, jnp.exp(masked - top), 0.0)
        return masked - top - jnp.log(jnp.sum(shifted, axis=1, keepdims=True))

    target_log = log_soft(target)
    student_log = log_soft(student_all)
    target_prob = jnp.where(member, jnp.exp(target_log), 0.0)
    terms = jnp.where(member, target_prob * (target_log - student_log), 0.0)
    div_column = jnp.sum(terms, axis=1, keepdims=True)
    eye8 = lax.broadcasted_iota(jnp.int32, (8, 8), 0) == lax.broadcasted_iota(jnp.int32, (8, 8), 1)
    div_ref[...] = jnp.sum(jnp.where(eye8, div_column, 0.0), axis=0, keepdims=True)

    @pl.when(c >= 6)
    def _():
        for d in range(1, 32):
            s_copy(d).wait_send()


def place(*refs):
    sems = refs[-1]
    half = (len(refs) - 1) // 2
    copies = [pltpu.make_async_copy(refs[i], refs[half + i], sems.at[i]) for i in range(half)]
    for copy in copies:
        copy.start()
    for copy in copies:
        copy.wait()


def local(
    student_hidden, w_query, w_keyval, w_out, norm_gain, student_head, teacher_query, teacher_keys, teacher_values,
    teacher_head, thread_lengths, list_index, relevance,
):
    vmem = pl.BlockSpec(memory_space=pltpu.VMEM)
    anywhere = pl.BlockSpec(memory_space=pl.ANY)
    dma = pltpu.SemaphoreType.DMA
    out, pooled, tscore, div = pl.pallas_call(
        kernel,
        out_shape=(
            pltpu.VMEM((ROWS, D), F32),
            pltpu.VMEM((4, D), F32),
            pltpu.VMEM((1, 4), F32),
            pltpu.VMEM((1, 8), F32),
        ),
        in_specs=[anywhere] * 13,
        out_specs=(vmem,) * 4,
        scratch_shapes=[
            pltpu.VMEM((ROWS, D), BF16),
            pltpu.VMEM((4, 2, 128, 256), BF16),
            pltpu.VMEM((4, 2, 128, 256), BF16),
            pltpu.VMEM((4, 2, 128, D), BF16),
            pltpu.VMEM((4, 2, 128, D), BF16),
            pltpu.VMEM((ROWS, 2048), BF16),
            pltpu.VMEM((ROWS, 2048), BF16),
            pltpu.VMEM((16, 4, 256, 128), BF16),
            pltpu.VMEM((2, 4, 256, 128), BF16),
            pltpu.VMEM((KV_HEADS, GROUPS, HD, ROWS), BF16),
            pltpu.VMEM((ROWS, D), BF16),
            pltpu.VMEM((HEADS, 1, ROWS), F32),
            pltpu.VMEM((HEADS, 1, ROWS), F32),
            pltpu.VMEM((HEADS, HD, ROWS), F32),
            pltpu.VMEM((2, 1, 384), F32),
            pltpu.VMEM((8, 1, 384), F32),
            pltpu.VMEM((1, 128), F32),
            pltpu.VMEM((6, 1, D), F32),
            pltpu.VMEM((1, D), F32),
            pltpu.VMEM((4, 1, D + 128), F32),
            pltpu.VMEM((16, 1, 128), F32),
            pltpu.VMEM((4, 1, D + 128), F32),
            pltpu.VMEM((8, 1, 128), F32),
            pltpu.VMEM((2, ROWS, 256), F32),
            pltpu.VMEM((1, D), F32),
            pltpu.VMEM((1, D), F32),
            pltpu.VMEM((4, 2048), BF16),
            pltpu.VMEM((1, 2048), F32),
            pltpu.SMEM((32,), jnp.int32),
            pltpu.VMEM((1, 32), jnp.int32),
            pltpu.VMEM((1, 32), jnp.int32),
            dma((14,)),
            dma((4, 29)),
            dma((4, 26)),
            dma((16, 4)),
            dma((8, 4)),
            dma((8, 4)),
            dma((4,)),
            dma((2, 4)),
            dma((2, 4)),
            dma((2,)),
            dma((9,)),
            dma,
            dma((6,)),
            dma((16,)),
            dma((4,)),
            dma((16,)),
            dma((16,)),
            dma((4,)),
            dma((4,)),
            dma((32,)),
            dma((8,)),
        ],
        compiler_params=pltpu.CompilerParams(
            collective_id=0, has_side_effects=True, vmem_limit_bytes=60 * 1024 * 1024
        ),
        cost_estimate=pl.CostEstimate(flops=10**10, bytes_accessed=8 * 2**20, transcendentals=8 * 10**6),
    )(
        student_hidden, w_keyval, w_query, w_out, norm_gain.reshape(1, -1), student_head.reshape(1, -1), teacher_query,
        teacher_keys, teacher_values, teacher_head.reshape(1, -1), thread_lengths, list_index.reshape(1, -1),
        relevance.reshape(1, -1),
    )
    out, pooled, tscore, div = pl.pallas_call(
        place,
        out_shape=tuple(jax.ShapeDtypeStruct(a.shape, a.dtype) for a in (out, pooled, tscore, div)),
        in_specs=[vmem] * 4,
        out_specs=(anywhere,) * 4,
        scratch_shapes=[dma((4,))],
        compiler_params=pltpu.CompilerParams(vmem_limit_bytes=16 * 1024 * 1024),
    )(out, pooled, tscore, div)
    return out, pooled, tscore.reshape(4), div.reshape(8)


def solution(mesh):
    return jax.shard_map(
        local,
        mesh=mesh,
        in_specs=(
            P(("dp", "ctx"), None), P("dp", None), P("dp", None), P("dp", None), P(), P(), P("dp", None),
            P(("dp", "ctx"), None), P(("dp", "ctx"), None), P(), P(), P(), P(),
        ),
        out_specs=(P(("dp", "ctx"), None), P("dp", None), P("dp"), P()),
        check_vma=False,
    )
```

```python
import functools

import jax
import jax.numpy as jnp
from jax import lax
from jax.experimental import pallas as pl
from jax.experimental.pallas import tpu as pltpu
from jax.sharding import PartitionSpec as P

HEADS = 8
KV_HEADS = 2
GROUPS = 4
HD = 128
T_HEADS = 16
ROWS = 256
D = 1024
CHIPS = 8
BIG = -1e30
F32 = jnp.float32
BF16 = jnp.bfloat16
SCALE = HD ** (-0.5)
LOG2E = 1.4426950408889634
MESH = pl.DeviceIdType.MESH


def kernel(
    hid_in, wkv_in, wq_in, wo_in, gain_in, shead_in, tq_in, tk_in, tv_in, thead_in, len_in, list_in, rel_in,
    out_ref, pooled_ref, tscore_ref, div_ref,
    hid, hidp, wk, wv, wq, wo, tk, tv, kvb, relay, qt, att, m_ref, l_ref, acc_ref,
    tsib, tbuf, trow, cbuf, cstage, pbuf, rbuf, ybuf, sbuf, kv_part,
    gain_ref, shead_ref, tq_ref, thead_ref, len_ref, list_ref, rel_ref,
    lsem, hsem, wsend, wrecv, kv_recv, kv_send, sib_send, rev_send, relay_recv, relay_send,
    t_send, t_recv, c_send, c_recv, p_send, p_recv, r_send, r_recv, y_send, y_recv, s_send, s_recv,
):
    dp = lax.axis_index("dp")
    ctx = lax.axis_index("ctx")
    x, zh = dp // 2, dp % 2
    y, pos = ctx // 16, ctx % 16
    c, k = pos // 2, pos % 2
    oz = 1 - zh
    other_dp = 2 * x + oz
    sib_ctx = ctx + 1 - 2 * k
    line = y * 16

    def remote(src, dst, ssem, rsem, to_dp, to_ctx):
        return pltpu.make_async_remote_copy(
            src_ref=src, dst_ref=dst, send_sem=ssem, recv_sem=rsem, device_id=(to_dp, to_ctx), device_id_type=MESH
        )

    def x_peer(d):
        return 2 * ((x + d) % 4) + zh

    def y_peer(d):
        return ((y + d) % 4) * 16 + pos

    thread = dp * 4 + y

    lane = 64 * k
    locals_ = [
        pltpu.make_async_copy(hid_in, hid, lsem.at[0]),
        pltpu.make_async_copy(tk_in, tk, lsem.at[1]),
        pltpu.make_async_copy(tv_in, tv, lsem.at[2]),
    ]
    weights = [(wkv_in.at[:, pl.ds(0, 256)], wk), (wkv_in.at[:, pl.ds(256, 256)], wv), (wq_in, wq), (wo_in, wo)]
    for i, (w_in, w) in enumerate(weights):
        locals_.append(
            pltpu.make_async_copy(w_in.at[pl.ds(lane, 64)], w.at[x, zh, pl.ds(lane, 64)], lsem.at[3 + i])
        )
    small = [
        (gain_in, gain_ref), (shead_in, shead_ref), (tq_in, tq_ref), (thead_in, thead_ref), (len_in, len_ref),
        (list_in, list_ref), (rel_in, rel_ref),
    ]
    small = [pltpu.make_async_copy(src, dst, lsem.at[7 + i]) for i, (src, dst) in enumerate(small)]
    for copy in [locals_[0]] + locals_[3:] + locals_[1:3]:
        copy.start()
    for copy in small:
        copy.start()

    barrier = pltpu.get_barrier_semaphore()

    def greet(to_dp, to_ctx):
        pl.semaphore_signal(barrier, inc=1, device_id=(to_dp, to_ctx), device_id_type=MESH)

    greet(dp, sib_ctx)
    for d in range(1, 4):
        greet(dp, y_peer(d))
        greet(x_peer(d), ctx)

    @pl.when(c < 7)
    def _():
        greet(dp, ctx + 2)

    @pl.when(c > 0)
    def _():
        greet(dp, ctx - 2)

    @pl.when(c == 0)
    def _():
        for j in range(4, 8):
            greet(other_dp, line + 2 * j + k)

    @pl.when(c == 7)
    def _():
        for j in range(5):
            greet(other_dp, line + 2 * j + k)

    @pl.when(jnp.logical_and(c >= 1, c <= 4))
    def _():
        greet(other_dp, line + 14 + k)

    @pl.when(jnp.logical_and(c >= 4, c <= 6))
    def _():
        greet(other_dp, line + k)

    @pl.when(c == 1)
    def _():
        greet(other_dp, line + 8 + k)

    @pl.when(c == 4)
    def _():
        greet(other_dp, line + 2 + k)

    def least(value, n):
        return (value + 8 - n) // 8

    @pl.when(c == 6)
    def _():
        for j in range(5):
            greet(dp, line + 2 * j + k)

    more = 3 - 2 * least(c, 1) - least(c, 2) + 2 * least(c, 4) - 2 * least(c, 5) + 4 * least(c, 7)
    pl.semaphore_wait(barrier, 10 + least(c, 1) - least(c, 5) - least(c, 7) + more)

    class Gather:
        def __init__(self, i):
            self.i = i
            self.w_in, self.w = weights[i]
            self.piece = 64 * k + 16 * y
            self.ring = i >= 2

        def sem(self, table, n):
            return table.at[self.i, n]

        def z_copy(self, j):
            w = self.w.at[x, zh, pl.ds(self.piece, 16)]
            return remote(
                self.w_in.at[pl.ds(self.piece, 16)], w, self.sem(wsend, j % 4), self.sem(wrecv, 0),
                other_dp, line + 2 * j + k,
            )

        def z_start(self):
            @pl.when(c == 0)
            def _():
                for j in range(4, 8):
                    self.z_copy(j).start()

            @pl.when(c == 7)
            def _():
                for j in range(4):
                    self.z_copy(j).start()

        def z_recv(self):
            w = self.w.at[x, oz, pl.ds(self.piece, 16)]
            remote(w, w, self.sem(wsend, 0), self.sem(wrecv, 0), other_dp, ctx).wait_recv()

        def own_part(self, at, first=0, rows=64):
            return self.w.at[(x + at) % 4, zh, pl.ds(lane + first, rows)]

        def own_copies(self):
            src = self.w_in.at[pl.ds(lane, 64)]
            hops = (1, 3) if self.ring else (1, 2, 3)
            return [
                remote(src, self.own_part(0), self.sem(wsend, 3 + d), self.sem(wrecv, d), x_peer(d), ctx) for d in hops
            ]

        def own_relays(self):
            left, right = self.own_part(3, 0, 32), self.own_part(1, 32, 32)
            return [
                remote(left, left, self.sem(wsend, 5), self.sem(wrecv, 2), x_peer(1), ctx),
                remote(right, right, self.sem(wsend, 15), self.sem(wrecv, 12), x_peer(3), ctx),
            ]

        def own_start(self):
            for copy in self.own_copies():
                copy.start()

        def arrived(self, w, n):
            remote(w, w, self.sem(wsend, 0), self.sem(wrecv, n), dp, ctx).wait_recv()

        def own_mid(self):
            relays = self.own_relays()
            self.arrived(self.own_part(3), 1)
            relays[0].start()
            self.arrived(self.own_part(1), 3)
            relays[1].start()

        def own_recv(self):
            if self.ring:
                self.arrived(self.own_part(2, 0, 32), 2)
                self.arrived(self.own_part(2, 32, 32), 12)
            else:
                for d in range(1, 4):
                    self.arrived(self.own_part(4 - d), d)

        def other_copy(self, d):
            w = self.w.at[x, oz, pl.ds(self.piece, 16)]
            return remote(w, w, self.sem(wsend, 6 + d), self.sem(wrecv, 3 + d), x_peer(d), ctx)

        def other_start(self):
            for d in range(1, 4):
                self.other_copy(d).start()

        def other_recv(self):
            for d in range(1, 4):
                self.arrived(self.w.at[(x + 4 - d) % 4, oz, pl.ds(self.piece, 16)], 3 + d)

        def y_part(self, at, first=0, count=4):
            return self.w.at[pl.ds(first, count), oz, pl.ds(64 * k + 16 * ((y + at) % 4), 16)]

        def y_copies(self):
            src = self.y_part(0)
            hops = (1, 3) if self.ring else (1, 2, 3)
            return [remote(src, src, self.sem(wsend, 9 + d), self.sem(wrecv, 6 + d), dp, y_peer(d)) for d in hops]

        def y_relays(self):
            left, right = self.y_part(3, 0, 2), self.y_part(1, 2, 2)
            return [
                remote(left, left, self.sem(wsend, 11), self.sem(wrecv, 8), dp, y_peer(1)),
                remote(right, right, self.sem(wsend, 16), self.sem(wrecv, 13), dp, y_peer(3)),
            ]

        def y_start(self):
            for copy in self.y_copies():
                copy.start()

        def y_mid(self):
            relays = self.y_relays()
            self.arrived(self.y_part(3), 7)
            relays[0].start()
            self.arrived(self.y_part(1), 9)
            relays[1].start()

        def y_recv(self):
            if self.ring:
                self.arrived(self.y_part(2, 0, 2), 8)
                self.arrived(self.y_part(2, 2, 2), 13)
            else:
                for d in range(1, 4):
                    self.arrived(self.y_part(4 - d), 6 + d)

        def sib_copy(self, half, n):
            w = self.w.at[:, half, pl.ds(lane, 64)]
            return remote(w, w, self.sem(wsend, 13 + n), self.sem(wrecv, 10 + n), dp, sib_ctx)

        def sib_recv(self, half, n):
            w = self.w.at[:, half, pl.ds(64 - lane, 64)]
            remote(w, w, self.sem(wsend, 0), self.sem(wrecv, 10 + n), dp, ctx).wait_recv()

        def finish(self):
            @pl.when(c == 0)
            def _():
                for j in range(4, 8):
                    self.z_copy(j).wait_send()

            @pl.when(c == 7)
            def _():
                for j in range(4):
                    self.z_copy(j).wait_send()

            copies = self.own_copies() + [self.other_copy(d) for d in range(1, 4)]
            copies += self.y_copies()
            for copy in copies + (self.own_relays() + self.y_relays() if self.ring else []):
                copy.wait_send()
            self.sib_copy(zh, 0).wait_send()
            self.sib_copy(oz, 1).wait_send()

    for copy in small:
        copy.wait()
    length = len_ref[thread]
    gk, gv, gq, go = (Gather(i) for i in range(4))

    gk.z_start()
    gk.own_start()
    gv.z_start()

    def hid_copy():
        return remote(hid_in, hidp, hsem.at[0], hsem.at[1], dp, ctx + 2)

    gives = jnp.logical_and(c >= 5, c <= 6)

    @pl.when(gives)
    def _():
        hid_copy().start()

    gk.z_recv()
    gk.other_start()
    gv.own_start()
    gv.z_recv()
    gv.other_start()
    gq.z_start()
    go.z_start()
    gk.own_recv()
    locals_[3].wait()
    gk.sib_copy(zh, 0).start()
    gk.other_recv()
    gk.y_start()
    gv.other_recv()
    gv.y_start()
    gv.own_recv()
    locals_[4].wait()
    gv.sib_copy(zh, 0).start()
    gq.own_start()
    locals_[0].wait()

    def project(rows, half, w):
        parts = [rows[:, pl.ds(pl.multiple_of((2 * i + half) * 128, 128), 128)] for i in range(4)]
        return jnp.dot(jnp.concatenate(parts, axis=1), w[:, half].reshape(512, 256), preferred_element_type=F32)

    gk.sib_recv(zh, 0)
    kv_part[0] = project(hid, zh, wk)
    gq.z_recv()
    gq.other_start()
    slot_row = lax.broadcasted_iota(jnp.int32, (4, 2048), 0) == y
    own_q = jnp.sum(jnp.where(slot_row, tq_ref[...].astype(F32), 0.0), axis=0, keepdims=True)
    head_of = lax.broadcasted_iota(jnp.int32, (T_HEADS, 2048), 1) // HD
    diagonal = head_of == lax.broadcasted_iota(jnp.int32, (T_HEADS, 2048), 0)
    q_heads = jnp.where(diagonal, own_q, 0.0).astype(BF16)
    locals_[1].wait()
    ts = lax.dot_general(q_heads, tk[...], (((1,), (1,)), ((), ())), preferred_element_type=F32) * SCALE
    t_valid = pos * ROWS + lax.broadcasted_iota(jnp.int32, (T_HEADS, ROWS), 1) < length
    ts = jnp.where(t_valid, ts, BIG)
    t_best = jnp.max(ts, axis=1, keepdims=True)
    t_weights = jnp.where(t_valid, jnp.exp(ts - t_best), 0.0)
    t_total = jnp.sum(t_weights, axis=1, keepdims=True)
    locals_[2].wait()
    t_out = jnp.dot(t_weights.astype(BF16), tv[...], preferred_element_type=F32)
    t_sum = jnp.sum(jnp.where(diagonal, t_out * thead_ref[...], 0.0), axis=1, keepdims=True)
    eye = lax.broadcasted_iota(jnp.int32, (T_HEADS, 128), 0) == lax.broadcasted_iota(jnp.int32, (T_HEADS, 128), 1)

    def row_of(column):
        return jnp.sum(jnp.where(eye, column, 0.0), axis=0, keepdims=True)

    tsib[k] = jnp.concatenate([row_of(t_best), row_of(t_total), row_of(t_sum)], axis=1)

    def t_copy():
        return remote(tsib.at[k], tsib.at[k], t_send.at[0], t_recv.at[0], dp, sib_ctx)

    def merged(rows):
        best = jnp.max(rows[:, :128], axis=0, keepdims=True)
        factor = jnp.exp(rows[:, :128] - best)
        sums = [jnp.sum(rows[:, n : n + 128] * factor, axis=0, keepdims=True) for n in (128, 256)]
        return jnp.concatenate([best] + sums, axis=1)

    def t_gather():
        return remote(tbuf.at[c], tbuf.at[c], t_send.at[1], t_recv.at[1 + c], dp, line + 12 + k)

    t_copy().start()

    gk.y_recv()
    gk.sib_copy(oz, 1).start()
    gv.sib_recv(zh, 0)
    kv_part[1] = project(hid, zh, wv)
    own = 2 * c + k

    def hand(b, q, ssem, to_ctx):
        ref = kvb.at[2 * b + k, q]
        return remote(ref, ref, ssem.at[b, q], kv_recv.at[2 * b + k, q], dp, to_ctx)

    def ring_copy(b, q):
        return hand(b, q, kv_send, ctx + 2)

    def back_copy(b, q):
        return hand(b, q, kv_send, ctx - 2)

    def sib_copy(b, q):
        return hand(b, q, sib_send, sib_ctx)

    def kv_wait(block, q):
        ref = kvb.at[block, q]
        remote(ref, ref, kv_send.at[0, 0], kv_recv.at[block, q], dp, ctx).wait_recv()

    def rev_copy(q):
        return remote(
            kvb.at[own, q], relay.at[c, q], rev_send.at[q], relay_recv.at[c, q], other_dp, line + 8 + k
        )

    def relay_copy(r, q):
        return remote(
            relay.at[r, q], kvb.at[2 * r + k, q], relay_send.at[r, q], kv_recv.at[2 * r + k, q], other_dp, line + 14 + k
        )

    def passes_on(b):
        gap = jnp.logical_or(jnp.logical_and(b == 0, c >= 4), jnp.logical_and(b == 1, c >= 6))
        gap = jnp.logical_or(gap, jnp.logical_and(b == c, c >= 5))
        return jnp.logical_and(c < 7, jnp.logical_not(gap))

    def passes_back(b):
        return jnp.logical_and(b == 0, c >= 6)

    def send_own(q):
        @pl.when(c < 5)
        def _():
            ring_copy(c, q).start()

        @pl.when(c == 0)
        def _():
            rev_copy(q).start()

        sib_copy(c, q).start()

    def send_before(q):
        @pl.when(c == 6)
        def _():
            ring_copy(c - 1, q).start()

        sib_copy(c - 1, q).start()

    def put_keys(block, keys, send):
        keys = keys.astype(BF16)
        for h in range(KV_HEADS):
            kvb[block, h] = keys[:, h * HD : (h + 1) * HD]
            send(h)

    def put_values(block, values, send):
        values = values.astype(BF16)
        for h in range(KV_HEADS):
            for part in range(2):
                piece = values[part * 128 : (part + 1) * 128, h * HD : (h + 1) * HD]
                kvb[block, 2 + h, pl.ds(part * 128, 128)] = piece.T
            send(2 + h)

    gk.sib_recv(oz, 1)
    put_keys(own, kv_part[0] + project(hid, oz, wk), send_own)
    gv.y_recv()
    gv.sib_copy(oz, 1).start()
    gv.sib_recv(oz, 1)
    put_values(own, kv_part[1] + project(hid, oz, wv), send_own)

    @pl.when(c >= 6)
    def _():
        remote(hidp, hidp, hsem.at[0], hsem.at[1], dp, ctx).wait_recv()
        put_keys(own - 2, project(hidp, zh, wk) + project(hidp, oz, wk), send_before)
        put_values(own - 2, project(hidp, zh, wv) + project(hidp, oz, wv), send_before)

    def block_at(s):
        last = -4 * least(s, 3) + 5 * least(s, 4) - least(s, 6) + 2 * least(s, 7)
        before = -2 * least(s, 4) + 3 * least(s, 5)
        return c - s + last * least(c, 7) + before * (least(c, 6) - least(c, 7))

    def forward(s, j):
        b = block_at(s)

        @pl.when(jnp.logical_and(s <= c, s > c // 6))
        def _():
            for q in (2 * j, 2 * j + 1):
                kv_wait(2 * b + k, q)

                @pl.when(passes_on(b))
                def _():
                    ring_copy(b, q).start()

                @pl.when(passes_back(b))
                def _():
                    back_copy(b, q).start()

                sib_copy(b, q).start()

    def relay_on(r, j):
        @pl.when(c == 4)
        def _():
            for q in (2 * j, 2 * j + 1):
                ref = relay.at[r, q]
                remote(ref, ref, rev_send.at[q], relay_recv.at[r, q], dp, ctx).wait_recv()
                relay_copy(r, q).start()

    def attend(b, h, diag):
        kp = jnp.concatenate([kvb[2 * b, h], kvb[2 * b + 1, h]], axis=0)
        v0, v1 = kvb[2 * b, 2 + h], kvb[2 * b + 1, 2 + h]
        vt = jnp.concatenate([v0[:128], v0[128:], v1[:128], v1[128:]], axis=1)
        queries = jnp.concatenate([qt[h, g] for g in range(GROUPS)], axis=1)
        wide = jnp.dot(kp, queries, preferred_element_type=F32) * (SCALE * LOG2E)
        for g in range(GROUPS):
            i = h * GROUPS + g
            s = wide[:, g * ROWS : (g + 1) * ROWS]
            if diag:
                key = lax.broadcasted_iota(jnp.int32, (2 * ROWS, ROWS), 0)
                row = lax.broadcasted_iota(jnp.int32, (2 * ROWS, ROWS), 1)
                s = jnp.where(key <= k * ROWS + row, s, BIG)
            best = jnp.max(s, axis=0, keepdims=True)
            if not diag:
                old = m_ref[i]
                best = jnp.maximum(old, best)
                carry = jnp.exp2(old - best)
            p = jnp.exp2(s - best)
            total = jnp.sum(p, axis=0, keepdims=True)
            out = jnp.dot(vt, p.astype(BF16), preferred_element_type=F32)
            m_ref[i] = best
            if diag:
                l_ref[i] = total
                acc_ref[i] = out
            else:
                l_ref[i] = l_ref[i] * carry + total
                acc_ref[i] = acc_ref[i] * carry + out

    gq.own_mid()
    gq.other_recv()
    gq.y_start()
    gq.own_recv()
    locals_[5].wait()
    gq.sib_copy(zh, 0).start()
    go.own_start()
    forward(1, 0)
    relay_on(0, 0)
    gq.y_mid()
    forward(1, 1)
    relay_on(0, 1)

    @pl.when(c == 1)
    def _():
        for q in range(4):
            rev_copy(q).start()

    go.z_recv()
    go.other_start()
    gq.y_recv()
    gq.sib_copy(oz, 1).start()
    forward(2, 0)
    gq.sib_recv(zh, 0)
    gq.sib_recv(oz, 1)
    query = jnp.dot(hid[...], wq[...].reshape(D, HEADS * HD), preferred_element_type=F32).astype(BF16)
    for i in range(HEADS):
        qt[i // GROUPS, i % GROUPS] = query[:, i * HD : (i + 1) * HD].T
    forward(2, 1)
    remote(tsib.at[1 - k], tsib.at[1 - k], t_send.at[0], t_recv.at[0], dp, ctx).wait_recv()
    tbuf[c] = merged(jnp.concatenate([tsib[0], tsib[1]], axis=0))

    @pl.when(c != 6)
    def _():
        t_gather().start()

    go.own_mid()
    for h in range(KV_HEADS):
        for q in (h, 2 + h):
            kv_wait(2 * c + 1 - k, q)
        attend(c, h, True)
    go.other_recv()
    go.y_start()

    def first_part(u):
        return u - 1 - (9 - u) * (1 - (u + 7) // 16)

    def part(a, carry):
        pair, h = a // 2, a % 2

        @pl.when(pair <= c)
        def _():
            b = block_at(pair)
            for j in range(2):
                kv_wait(2 * b + 1 - k, 2 * j + h)
            attend(b, h, False)

        return carry

    def step(s, carry):
        for j in range(2):
            forward(s, j)

            @pl.when(s == 3)
            def _():
                relay_on(1, j)

            u = 2 * s + j
            lax.fori_loop(first_part(u), first_part(u + 1), part, 0)

        @pl.when(s == 3)
        def _():
            go.own_recv()
            locals_[6].wait()
            go.sib_copy(zh, 0).start()

        @pl.when(s == 4)
        def _():
            go.y_mid()

        @pl.when(s == 5)
        def _():
            go.y_recv()
            go.sib_copy(oz, 1).start()

        return carry

    lax.fori_loop(3, 8, step, 0)
    part(15, 0)

    for i in range(HEADS):
        att[:, i * HD : (i + 1) * HD] = (acc_ref[i] / l_ref[i]).astype(BF16).T
    go.sib_recv(zh, 0)
    go.sib_recv(oz, 1)
    hidden = hid[...].astype(F32) + jnp.dot(att[...], wo[...].reshape(D, D), preferred_element_type=F32)
    valid = pos * ROWS + lax.broadcasted_iota(jnp.int32, (ROWS, 1), 0) < length
    rate = jnp.where(valid, lax.rsqrt(jnp.mean(hidden * hidden, axis=1, keepdims=True) + 1e-05), 0.0)
    part = jnp.sum(hidden * rate, axis=0, keepdims=True) * gain_ref[...]
    out_ref[...] = jnp.where(valid, hidden, 0.0)

    def chain_copy():
        return remote(cstage, cbuf.at[c], c_send, c_recv.at[c], dp, line + 12 + k)

    cstage[...] = part

    @pl.when(c <= 5)
    def _():
        chain_copy().start()

    root = 2 * (c - 6) + k
    lanes = lax.broadcasted_iota(jnp.int32, (1, 128), 1)

    @pl.when(c == 7)
    def _():
        trow[...] = jnp.zeros_like(trow)

    @pl.when(c == 6)
    def _():
        for i in (0, 1, 2, 3, 4, 5, 7):
            remote(tbuf.at[i], tbuf.at[i], t_send.at[0], t_recv.at[1 + i], dp, ctx).wait_recv()
        stats = merged(tbuf[...].reshape(8, 384))
        in_heads = lanes < T_HEADS
        above, below = stats[:, 256:], jnp.where(in_heads, stats[:, 128:256], 1.0)
        t_score = jnp.sum(jnp.where(in_heads, above / below, 0.0), axis=1, keepdims=True)
        trow[...] = jnp.where(k == 0, jnp.broadcast_to(t_score, (1, 128)), 0.0)
        for i in range(6):
            remote(cstage, cbuf.at[i], c_send, c_recv.at[i], dp, ctx).wait_recv()
        cstage[...] = cstage[...] + jnp.sum(cbuf[...].reshape(6, D), axis=0, keepdims=True)

    def p_copy(d):
        return remote(pbuf.at[root], pbuf.at[root], p_send.at[d], p_recv.at[root], dp, line + (pos + d) % 16)

    spot = 4 * x + y

    def r_copy(d):
        there = (spot + d) % 16
        return remote(
            rbuf.at[spot], rbuf.at[spot], r_send.at[d], r_recv.at[d], 2 * (there // 4) + zh, 16 * (there % 4) + pos
        )

    deep = 16 * zh + pos

    def s_copy(d):
        there = (deep + d) % 32
        slot = sbuf.at[4 * zh + root]
        return remote(slot, slot, s_send.at[d], s_recv.at[4 * zh + root], 2 * x + there // 16, line + there % 16)

    @pl.when(c >= 6)
    def _():
        mean = cstage[...] / length.astype(F32)
        student = jnp.sum(mean * shead_ref[...], axis=1, keepdims=True)
        rbuf[spot] = jnp.where(lanes == thread, student, 0.0) + jnp.where(lanes == 64 + thread, trow[...], 0.0)
        for d in sorted(range(1, 16), key=lambda d: -min(d // 4, 4 - d // 4) - min(d % 4, 4 - d % 4)):
            r_copy(d).start()
        pbuf[root] = jnp.concatenate([mean, trow[...]], axis=1)
        for d in range(1, 16):
            p_copy(d).start()
        for d in range(1, 16):
            ref = rbuf.at[(spot + 16 - d) % 16]
            remote(ref, ref, r_send.at[0], r_recv.at[d], dp, ctx).wait_recv()
        sbuf[4 * zh + root] = jnp.sum(rbuf[...].reshape(16, 128), axis=0, keepdims=True)
        for d in sorted(range(1, 32), key=lambda d: abs(d - 16)):
            s_copy(d).start()

    for r in range(4):

        @pl.when(pos != 12 + r)
        def _():
            ref = pbuf.at[r]
            remote(ref, ref, p_send.at[0], p_recv.at[r], dp, ctx).wait_recv()

    ybuf[y] = (pbuf[0] + pbuf[1]) + (pbuf[2] + pbuf[3])

    def y_copy(d):
        return remote(ybuf.at[y], ybuf.at[y], y_send.at[d], y_recv.at[d], dp, y_peer(d))

    for d in range(1, 4):
        y_copy(d).start()

    def sent(b, carry):
        for q in range(4):

            @pl.when(jnp.logical_or(passes_on(b), passes_back(b)))
            def _():
                ring_copy(b, q).wait_send()

            sib_copy(b, q).wait_send()
        return carry

    lax.fori_loop(0, c + 1, sent, 0)

    @pl.when(c <= 1)
    def _():
        for q in range(4):
            rev_copy(q).wait_send()

    @pl.when(gives)
    def _():
        hid_copy().wait_send()

    @pl.when(c == 4)
    def _():
        for r in range(2):
            for q in range(4):
                relay_copy(r, q).wait_send()

    for gather in (gk, gv, gq, go):
        gather.finish()
    t_copy().wait_send()

    @pl.when(c != 6)
    def _():
        t_gather().wait_send()

    @pl.when(c <= 5)
    def _():
        chain_copy().wait_send()

    @pl.when(c >= 6)
    def _():
        for d in range(1, 16):
            r_copy(d).wait_send()
            p_copy(d).wait_send()

    for d in range(1, 4):
        ref = ybuf.at[(y + 4 - d) % 4]
        remote(ref, ref, y_send.at[0], y_recv.at[d], dp, ctx).wait_recv()
    rows = jnp.concatenate([ybuf[i] for i in range(4)], axis=0)
    pooled_ref[...] = rows[:, :D]
    eye4 = lax.broadcasted_iota(jnp.int32, (4, 4), 0) == lax.broadcasted_iota(jnp.int32, (4, 4), 1)
    tscore_ref[...] = jnp.sum(jnp.where(eye4, rows[:, D : D + 4], 0.0), axis=0, keepdims=True)
    for d in range(1, 4):
        y_copy(d).wait_send()

    for r in range(8):

        @pl.when(deep != 12 + r + 12 * (r // 4))
        def _():
            ref = sbuf.at[r]
            remote(ref, ref, s_send.at[0], s_recv.at[r], dp, ctx).wait_recv()

    every = jnp.sum(sbuf[...].reshape(8, 128), axis=0, keepdims=True)
    threads = list_ref.shape[1]
    student_all, teacher_all = every[:, :threads], every[:, 64 : 64 + threads]
    target = teacher_all + rel_ref[...].astype(F32)
    member = lax.broadcasted_iota(jnp.int32, (8, threads), 0) == list_ref[...]

    def log_soft(logits):
        masked = jnp.where(member, logits, BIG)
        top = jnp.max(masked, axis=1, keepdims=True)
        shifted = jnp.where(member, jnp.exp(masked - top), 0.0)
        return masked - top - jnp.log(jnp.sum(shifted, axis=1, keepdims=True))

    target_log = log_soft(target)
    student_log = log_soft(student_all)
    target_prob = jnp.where(member, jnp.exp(target_log), 0.0)
    terms = jnp.where(member, target_prob * (target_log - student_log), 0.0)
    div_column = jnp.sum(terms, axis=1, keepdims=True)
    eye8 = lax.broadcasted_iota(jnp.int32, (8, 8), 0) == lax.broadcasted_iota(jnp.int32, (8, 8), 1)
    div_ref[...] = jnp.sum(jnp.where(eye8, div_column, 0.0), axis=0, keepdims=True)

    @pl.when(c >= 6)
    def _():
        for d in range(1, 32):
            s_copy(d).wait_send()


def place(*refs):
    sems = refs[-1]
    half = (len(refs) - 1) // 2
    copies = [pltpu.make_async_copy(refs[i], refs[half + i], sems.at[i]) for i in range(half)]
    for copy in copies:
        copy.start()
    for copy in copies:
        copy.wait()


def local(
    student_hidden, w_query, w_keyval, w_out, norm_gain, student_head, teacher_query, teacher_keys, teacher_values,
    teacher_head, thread_lengths, list_index, relevance,
):
    vmem = pl.BlockSpec(memory_space=pltpu.VMEM)
    anywhere = pl.BlockSpec(memory_space=pl.ANY)
    dma = pltpu.SemaphoreType.DMA
    out, pooled, tscore, div = pl.pallas_call(
        kernel,
        out_shape=(
            pltpu.VMEM((ROWS, D), F32),
            pltpu.VMEM((4, D), F32),
            pltpu.VMEM((1, 4), F32),
            pltpu.VMEM((1, 8), F32),
        ),
        in_specs=[anywhere] * 13,
        out_specs=(vmem,) * 4,
        scratch_shapes=[
            pltpu.VMEM((ROWS, D), BF16),
            pltpu.VMEM((ROWS, D), BF16),
            pltpu.VMEM((4, 2, 128, 256), BF16),
            pltpu.VMEM((4, 2, 128, 256), BF16),
            pltpu.VMEM((4, 2, 128, D), BF16),
            pltpu.VMEM((4, 2, 128, D), BF16),
            pltpu.VMEM((ROWS, 2048), BF16),
            pltpu.VMEM((ROWS, 2048), BF16),
            pltpu.VMEM((16, 4, 256, 128), BF16),
            pltpu.VMEM((2, 4, 256, 128), BF16),
            pltpu.VMEM((KV_HEADS, GROUPS, HD, ROWS), BF16),
            pltpu.VMEM((ROWS, D), BF16),
            pltpu.VMEM((HEADS, 1, ROWS), F32),
            pltpu.VMEM((HEADS, 1, ROWS), F32),
            pltpu.VMEM((HEADS, HD, ROWS), F32),
            pltpu.VMEM((2, 1, 384), F32),
            pltpu.VMEM((8, 1, 384), F32),
            pltpu.VMEM((1, 128), F32),
            pltpu.VMEM((6, 1, D), F32),
            pltpu.VMEM((1, D), F32),
            pltpu.VMEM((4, 1, D + 128), F32),
            pltpu.VMEM((16, 1, 128), F32),
            pltpu.VMEM((4, 1, D + 128), F32),
            pltpu.VMEM((8, 1, 128), F32),
            pltpu.VMEM((2, ROWS, 256), F32),
            pltpu.VMEM((1, D), F32),
            pltpu.VMEM((1, D), F32),
            pltpu.VMEM((4, 2048), BF16),
            pltpu.VMEM((1, 2048), F32),
            pltpu.SMEM((32,), jnp.int32),
            pltpu.VMEM((1, 32), jnp.int32),
            pltpu.VMEM((1, 32), jnp.int32),
            dma((14,)),
            dma((2,)),
            dma((4, 17)),
            dma((4, 14)),
            dma((16, 4)),
            dma((8, 4)),
            dma((8, 4)),
            dma((4,)),
            dma((2, 4)),
            dma((2, 4)),
            dma((2,)),
            dma((9,)),
            dma,
            dma((6,)),
            dma((16,)),
            dma((4,)),
            dma((16,)),
            dma((16,)),
            dma((4,)),
            dma((4,)),
            dma((32,)),
            dma((8,)),
        ],
        compiler_params=pltpu.CompilerParams(
            collective_id=0, has_side_effects=True, vmem_limit_bytes=60 * 1024 * 1024
        ),
        cost_estimate=pl.CostEstimate(flops=10**10, bytes_accessed=8 * 2**20, transcendentals=8 * 10**6),
    )(
        student_hidden, w_keyval, w_query, w_out, norm_gain.reshape(1, -1), student_head.reshape(1, -1), teacher_query,
        teacher_keys, teacher_values, teacher_head.reshape(1, -1), thread_lengths, list_index.reshape(1, -1),
        relevance.reshape(1, -1),
    )
    out, pooled, tscore, div = pl.pallas_call(
        place,
        out_shape=tuple(jax.ShapeDtypeStruct(a.shape, a.dtype) for a in (out, pooled, tscore, div)),
        in_specs=[vmem] * 4,
        out_specs=(anywhere,) * 4,
        scratch_shapes=[dma((4,))],
        compiler_params=pltpu.CompilerParams(vmem_limit_bytes=16 * 1024 * 1024),
    )(out, pooled, tscore, div)
    return out, pooled, tscore.reshape(4), div.reshape(8)


def solution(mesh):
    return jax.shard_map(
        local,
        mesh=mesh,
        in_specs=(
            P(("dp", "ctx"), None), P("dp", None), P("dp", None), P("dp", None), P(), P(), P("dp", None),
            P(("dp", "ctx"), None), P(("dp", "ctx"), None), P(), P(), P(), P(),
        ),
        out_specs=(P(("dp", "ctx"), None), P("dp", None), P("dp"), P()),
        check_vma=False,
    )
```
